32 devices in a mesh: hap: 4 (over z), pos: 8 (over y, x, core).
Axes of the slice: x: 2, y: 2, z: 4, core: 2. Of those that a mesh axis runs over, the one named last changes fastest.
Arguments:
- haplo_rows: bfloat16 [12, 2048, 1024], P('hap', 'pos'), may hold values from -6 to 6
- norm_gain: float32 [1024], replicated, may hold values from 0.25 to 1.75
- query_row: bfloat16 [1024, 1024], replicated, may hold values from -0.1875 to 0.1875
- key_row: bfloat16 [1024, 1024], replicated, may hold values from -0.1875 to 0.1875
- value_row: bfloat16 [1024, 1024], replicated, may hold values from -0.1875 to 0.1875
- out_row: bfloat16 [1024, 1024], replicated, may hold values from -0.1875 to 0.1875
- head_gain: float32 [1024], replicated, may hold values from 0.25 to 1.75
- query_col: bfloat16 [1024, 1024], replicated, may hold values from -0.1875 to 0.1875
- key_col: bfloat16 [1024, 1024], replicated, may hold values from -0.1875 to 0.1875
- value_col: bfloat16 [1024, 1024], replicated, may hold values from -0.1875 to 0.1875
- out_col: bfloat16 [1024, 1024], replicated, may hold values from -0.1875 to 0.1875
- temper: float32 [16], replicated, may hold values from 4 to 16
Outputs:
- updated: bfloat16 [12, 2048, 1024], P('hap', 'pos')
The draws below stay inside these ranges and needn't reach their ends.
All inputs are finite; a program needn't handle non-finite values.
Results may differ from the reference program's by a relative error of at most 0.01.
Values may be sent and summed in bfloat16 or wider, within the bound.
No kernel may reach another device: no remote copies, remote signals or barrier semaphores. Data moves between devices by JAX's collectives and lax.ppermute only.
A program may use at most 128 MiB of HBM per device.

```python
import math
import jax
import jax.numpy as jnp
from jax import lax

D = 1024
H = 16
E = 64
P_DEV = 256
R = 12
L = 2048


def steps_of(key, extent, split, least, high):
    def one(dim, blocks):
        heights = jax.random.uniform(jax.random.fold_in(jax.random.fold_in(key, 6), dim), (blocks,), jnp.float32, least / len(split), high / len(split))
        return jnp.repeat(jnp.exp(heights), extent[dim] // blocks).reshape((-1,) + (1,) * (len(extent) - dim - 1))

    factor_of = one(*split[0])
    for cut in split[1:]:
        factor_of = factor_of * one(*cut)
    return factor_of


def gaussian(key, extent, spread, bound, shards=(), dtype=jnp.bfloat16):
    values = spread * jax.random.normal(key, extent, jnp.float32)
    if shards:
        values = values * steps_of(key, extent, shards, -0.22, 0.18)
    return jnp.clip(values, -bound, bound).astype(dtype)


def setup_inputs(seed: int = 0) -> dict:
    key_list = jax.random.split(jax.random.key(seed), 13)
    haplo_rows = gaussian(key_list[0], (R, L, D), 1.0, 6.0, ((0, 4), (1, 8)))
    norm_gain = jnp.clip(1.0 + 0.15 * jax.random.normal(key_list[1], (D,), jnp.float32), 0.25, 1.75)
    query_row = gaussian(key_list[2], (D, D), D ** -0.5, 0.1875)
    key_row = gaussian(key_list[3], (D, D), D ** -0.5, 0.1875)
    value_row = gaussian(key_list[4], (D, D), D ** -0.5, 0.1875)
    out_row = gaussian(key_list[5], (D, D), D ** -0.5, 0.1875)
    head_gain = jnp.clip(1.0 + 0.15 * jax.random.normal(key_list[6], (D,), jnp.float32), 0.25, 1.75)
    query_col = gaussian(key_list[7], (D, D), D ** -0.5, 0.1875)
    key_col = gaussian(key_list[8], (D, D), D ** -0.5, 0.1875)
    value_col = gaussian(key_list[9], (D, D), D ** -0.5, 0.1875)
    out_col = gaussian(key_list[10], (D, D), D ** -0.5, 0.1875)
    temper = jnp.clip(jnp.exp(jax.random.uniform(key_list[11], (H,), jnp.float32, math.log(4.0), math.log(16.0))), 4.0, 16.0)
    return dict(haplo_rows=haplo_rows, norm_gain=norm_gain, query_row=query_row, key_row=key_row, value_row=value_row, out_row=out_row, head_gain=head_gain, query_col=query_col, key_col=key_col, value_col=value_col, out_col=out_col, temper=temper)


def features(u):
    return jnp.concatenate([jax.nn.elu(u) + 1.0, jax.nn.elu(-u) + 1.0], axis=-1)

def unit_heads(u):
    values = u.astype(jnp.float32)
    return values * lax.rsqrt(lax.optimization_barrier(jnp.sum(values * values, axis=-1, keepdims=True)) + 1e-06)

def reference(haplo_rows, norm_gain, query_row, key_row, value_row, out_row, head_gain, query_col, key_col, value_col, out_col, temper):
    high = lax.Precision.HIGHEST
    inputs = haplo_rows.astype(jnp.float32)
    normed = (inputs * lax.rsqrt(lax.optimization_barrier(jnp.mean(inputs * inputs, axis=-1, keepdims=True)) + 1e-06) * norm_gain).astype(jnp.bfloat16)
    flat = normed.reshape(R * L, D)

    def project(weight):
        return jnp.dot(flat, weight, preferred_element_type=jnp.float32).astype(jnp.bfloat16).reshape(R, L, H, E)
    q_row = project(query_row)
    k_row = project(key_row)
    v_row = project(value_row)
    fq = features(q_row.astype(jnp.float32)).astype(jnp.bfloat16)
    fk = features(k_row.astype(jnp.float32)).astype(jnp.bfloat16)
    state = jnp.einsum('rlhf,rlhe->rhfe', fk.astype(jnp.float32), v_row.astype(jnp.float32), precision=high)
    along = jnp.einsum('rlhf,rhfe->rlhe', fq.astype(jnp.float32), state, precision=high)
    along = along * lax.rsqrt(lax.optimization_barrier(jnp.mean(along * along, axis=-1, keepdims=True)) + 1e-06)
    row_mixed = (along.reshape(R, L, D) * head_gain).astype(jnp.bfloat16)
    row_out = jnp.dot(row_mixed.reshape(R * L, D), out_row, preferred_element_type=jnp.float32).reshape(R, L, D)
    q_col = project(query_col)
    k_col = project(key_col)
    v_col = project(value_col)
    qn = (unit_heads(q_col) * temper[:, None]).astype(jnp.bfloat16)
    kn = unit_heads(k_col).astype(jnp.bfloat16)
    blocks = L // P_DEV

    def split_blocks(array):
        return array.reshape(R, blocks, P_DEV, H, E).transpose(1, 0, 2, 3, 4)

    def one_block(operands):
        query_b, key_b, value_b = operands
        scores = jnp.einsum('aphe,bphe->phab', query_b.astype(jnp.float32), key_b.astype(jnp.float32), precision=high)
        weight = jnp.exp(scores).astype(jnp.bfloat16)
        weight = lax.optimization_barrier(weight).astype(jnp.float32)
        total = lax.optimization_barrier(jnp.sum(weight, axis=-1))
        summed = jnp.einsum('phab,bphe->aphe', weight, value_b.astype(jnp.float32), precision=high)
        return (summed / jnp.transpose(total, (2, 0, 1))[..., None]).astype(jnp.bfloat16)
    mixed_blocks = lax.map(one_block, (split_blocks(qn), split_blocks(kn), split_blocks(v_col)))
    col_mixed = mixed_blocks.transpose(1, 0, 2, 3, 4).reshape(R * L, D)
    col_out = jnp.dot(col_mixed, out_col, preferred_element_type=jnp.float32).reshape(R, L, D)
    return (inputs + row_out + col_out).astype(jnp.bfloat16)
```

```python
import functools

import jax
import jax.numpy as jnp
from jax import lax
from jax.experimental import pallas as pl
from jax.experimental.pallas import tpu as pltpu
from jax.sharding import PartitionSpec as P

EPS = 1e-06
LANES = 128
TILE = 16
F32 = jnp.float32
BF16 = jnp.bfloat16
VMEM_LIMIT = 40 * 1024 * 1024
COLUMN_COSTS = (200, 30)
FINISH_COSTS = (30, 0)


def last_dims(left, right):
    return lax.dot_general(left, right, (((1,), (1,)), ((), ())), preferred_element_type=F32)


def first_dims(left, right):
    return lax.dot_general(left, right, (((0,), (0,)), ((), ())), preferred_element_type=F32)


def plain(left, right):
    return jnp.dot(left, right, preferred_element_type=F32)


def lane_of(shape):
    return lax.broadcasted_iota(jnp.int32, shape, len(shape) - 1)


def group_ones(size, head_dim):
    rows = lax.broadcasted_iota(jnp.int32, (size, size), 0) // head_dim
    cols = lax.broadcasted_iota(jnp.int32, (size, size), 1) // head_dim
    return jnp.where(rows == cols, 1.0, 0.0).astype(BF16)


def head_square_sums(values, ones):
    size = ones.shape[0]
    parts = []
    for start in range(0, values.shape[1], size):
        piece = values[:, start : start + size]
        square = piece * piece
        high = square.astype(BF16)
        low = (square - high.astype(F32)).astype(BF16)
        parts.append(plain(high, ones) + plain(low, ones))
    return jnp.concatenate(parts, axis=1) if len(parts) > 1 else parts[0]


def feature_pair(values):
    small = jnp.exp(-jnp.abs(values))
    up = values > 0
    plus = jnp.where(up, values + 1.0, small).astype(BF16)
    minus = jnp.where(up, small, 1.0 - values).astype(BF16)
    return plus, minus


def pack_kernel(places, place_ref, rows_ref, gain_ref, *outs):
    z = place_ref[0]
    gain = gain_ref[...]
    for (c, k), (index, slot) in places.items():
        block = rows_ref[0, z ^ k, c].astype(F32)
        scale = lax.rsqrt(jnp.mean(block * block, axis=-1, keepdims=True) + EPS)
        outs[index][slot, 0] = (block * scale * gain).astype(BF16)


def row_kernel(head_dim, places, *refs):
    wq_ref, wk_ref, wv_ref, q_ref, state_ref = refs[-5:]
    rows = jnp.concatenate([refs[index][slot, 0] for index, slot in places.values()], axis=0)
    keys = plain(rows, wk_ref[...]).astype(BF16)
    values = plain(rows, wv_ref[...]).astype(BF16)
    first_head = lane_of((head_dim, 2 * LANES)) % LANES < head_dim
    for pair in range(keys.shape[1] // LANES):
        lower = pair * LANES
        plus, minus = feature_pair(keys[:, lower : lower + LANES].astype(F32))
        features = jnp.concatenate([plus, minus], axis=1)
        state = first_dims(values[:, lower : lower + LANES], features)
        folded = jnp.where(first_head, state[:head_dim], state[head_dim:])
        state_ref[pair, 0] = folded.astype(BF16)
    q_ref[0] = plain(rows, wq_ref[...]).astype(BF16)


def along_kernel(head_dim, order, place_ref, rows_ref, q_ref, state_ref, gain_ref, wo_ref, out_ref, mixed):
    z = place_ref[0]
    first_head = lane_of((head_dim, 2 * LANES)) % LANES < head_dim
    ones = group_ones(2 * LANES, head_dim)
    alongs = []
    for pair in range(state_ref.shape[0]):
        lower = pair * LANES
        plus, minus = feature_pair(q_ref[0, :, lower : lower + LANES].astype(F32))
        features = jnp.concatenate([plus, minus], axis=1)
        folded = state_ref[pair, 0]
        none = jnp.zeros_like(folded)
        state = jnp.concatenate(
            [jnp.where(first_head, folded, none), jnp.where(first_head, none, folded)], axis=0
        )
        alongs.append(last_dims(features, state))
        if pair % 2 == 1:
            lower -= LANES
            wide = jnp.concatenate(alongs[-2:], axis=1)
            mean = head_square_sums(wide, ones) * (1.0 / head_dim)
            scaled = wide * lax.rsqrt(mean + EPS) * gain_ref[:, lower : lower + 2 * LANES]
            mixed[:, lower : lower + 2 * LANES] = scaled.astype(BF16)
    row_out = plain(mixed[...], wo_ref[...])
    depth = rows_ref.shape[3]
    for i, (c, k) in enumerate(order):
        out_ref[0, i] = rows_ref[0, z ^ k, c].astype(F32) + row_out[i * depth : (i + 1) * depth]


def column_kernel(head_dim, count, temper_ref, wq_ref, wk_ref, wv_ref, *refs):
    blocks = refs[:count]
    outs = refs[-3 - count : -3]
    q_all, k_all, v_all = refs[-3:]
    _one, haps, depth, width = blocks[0].shape
    rows = jnp.concatenate([block[0, r] for block in blocks for r in range(haps)], axis=0)
    shape = q_all.shape
    ones = group_ones(2 * LANES, head_dim)
    q = plain(rows, wq_ref[...]).astype(BF16).astype(F32)
    q = q * lax.rsqrt(head_square_sums(q, ones) + EPS) * temper_ref[...]
    q_all[...] = q.astype(BF16).reshape(shape)
    k = plain(rows, wk_ref[...]).astype(BF16).astype(F32)
    k = k * lax.rsqrt(head_square_sums(k, ones) + EPS)
    k_all[...] = k.astype(BF16).reshape(shape)
    v_all[...] = plain(rows, wv_ref[...]).astype(BF16).reshape(shape)
    all_haps = shape[0]
    many = all_haps * TILE
    same = (
        lax.broadcasted_iota(jnp.int32, (many, many), 0) % TILE
        == lax.broadcasted_iota(jnp.int32, (many, many), 1) % TILE
    )
    first_head = lane_of((many, LANES)) < head_dim
    none = jnp.zeros((many, LANES), BF16)
    one = jnp.ones((many, LANES), BF16)
    for start in range(0, depth, TILE):
        for lower in range(0, width, LANES):
            at = (slice(None), slice(start, start + TILE), slice(lower, lower + LANES))
            query = q_all[at].reshape(many, LANES)
            key = k_all[at].reshape(many, LANES)
            value = v_all[at].reshape(many, LANES)
            score_a = last_dims(jnp.where(first_head, query, none), key)
            score_b = last_dims(jnp.where(first_head, none, query), key)
            weight_a = jnp.where(same, jnp.exp(score_a), 0.0).astype(BF16)
            weight_b = jnp.where(same, jnp.exp(score_b), 0.0).astype(BF16)
            sum_a = plain(weight_a, jnp.where(first_head, value, one))
            sum_b = plain(weight_b, jnp.where(first_head, one, value))
            summed = jnp.where(first_head, sum_a, sum_b)
            total = pltpu.roll(jnp.where(first_head, sum_b, sum_a), head_dim, 1)
            result = (summed / total).astype(BF16).reshape(all_haps, TILE, LANES)
            for k in range(count):
                outs[k][0, :, start : start + TILE, lower : lower + LANES] = result[
                    k * haps : (k + 1) * haps
                ]


def finish_kernel(pieces, order, place_ref, acc_ref, wo_ref, *refs):
    mixed = refs[: len(pieces)]
    out_ref, acc, result, acc_sems, out_sems = refs[-5:]
    z = place_ref[0]
    _one, haps, depth, _width = mixed[0].shape
    loads = [
        pltpu.make_async_copy(acc_ref.at[:, order.index(piece)], acc.at[i], acc_sems.at[i])
        for i, piece in enumerate(pieces)
    ]
    for load in loads:
        load.start()
    flat = jnp.concatenate([block[0, r] for block in mixed for r in range(haps)], axis=0)
    col_out = plain(flat, wo_ref[...])
    stores = []
    for i, (c, k) in enumerate(pieces):
        loads[i].wait()
        for r in range(haps):
            lower = (i * haps + r) * depth
            result[i, r] = (acc[i, r] + col_out[lower : lower + depth]).astype(BF16)
        store = pltpu.make_async_copy(result.at[i], out_ref.at[:, z ^ k, c], out_sems.at[i])
        store.start()
        stores.append(store)
    for store in stores:
        store.wait()


def whole(array):
    zeros = (0,) * array.ndim
    return pl.BlockSpec(array.shape, lambda *_: zeros)


def once(array):
    zeros = (0,) * array.ndim
    return pl.BlockSpec(array.shape, lambda *_: zeros, pipeline_mode=pl.Buffered(1))


SCALARS = pl.BlockSpec(memory_space=pltpu.SMEM)
PARAMS = pltpu.CompilerParams(vmem_limit_bytes=VMEM_LIMIT)


def cost(micros):
    return pl.CostEstimate(flops=int(micros * 1e9), bytes_accessed=1, transcendentals=0)


def local(
    sizes,
    haplo_rows,
    norm_gain,
    query_row,
    key_row,
    value_row,
    out_row,
    head_gain,
    query_col,
    key_col,
    value_col,
    out_col,
    temper,
):
    n, m = sizes
    haps, length, width = haplo_rows.shape
    heads = temper.shape[0]
    head_dim = width // heads
    owned = length // n
    chunks = 2 if owned % (2 * TILE) == 0 else 1
    depth = owned // chunks
    pairs = width // LANES
    place = lax.axis_index("hap").astype(jnp.int32)[None]
    rows5 = haplo_rows.reshape(haps, n, chunks, depth, width)
    gain_flat = norm_gain[None, :]
    head_gain_flat = head_gain[None, :]
    temper_flat = jnp.repeat(temper, head_dim)[None, :]
    anywhere = pl.BlockSpec(memory_space=pl.ANY)

    def exchange(array, k):
        return lax.ppermute(array, "hap", [(i, i ^ k) for i in range(n)])

    order = [(c, k) for c in range(chunks) for k in range(n)]
    places, lengths = {}, []
    for c, k in order:
        if k == 1 and c > 0:
            places[c, k] = (places[0, 1][0], c)
        else:
            places[c, k] = (len(lengths), 0)
            lengths.append(chunks if k == 1 else 1)
    shapes = [jax.ShapeDtypeStruct((many, haps, depth, width), BF16) for many in lengths]
    hap_specs = [
        pl.BlockSpec((many, 1, depth, width), lambda r: (0, r, 0, 0)) for many in lengths
    ]
    rows_spec = pl.BlockSpec((1, n, chunks, depth, width), lambda r: (r, 0, 0, 0, 0))

    def piece_spec(c, k):
        slot = places[c, k][1]
        return pl.BlockSpec((1, haps, depth, width), lambda *_: (slot, 0, 0, 0))

    normed = pl.pallas_call(
        functools.partial(pack_kernel, places),
        grid=(haps,),
        in_specs=[SCALARS, rows_spec, whole(gain_flat)],
        out_specs=hap_specs,
        out_shape=shapes,
        compiler_params=PARAMS,
        cost_estimate=cost(0),
        name="pack",
    )(place, rows5, gain_flat)

    def send_all(arrays):
        got = {}
        sent = list(arrays)
        for c, k in order[1:] if n > 1 else []:
            index, slot = places[c, k]
            if k > 0 and slot == 0:
                sent[index] = exchange(arrays[index], k)
        return sent

    arrived = send_all(normed)

    full_rows = jax.ShapeDtypeStruct((haps, length, width), BF16)
    row_spec = pl.BlockSpec((1, length, width), lambda r: (r, 0, 0))
    state_spec = pl.BlockSpec((pairs, 1, head_dim, 2 * LANES), lambda r: (0, r, 0, 0))
    state_shape = (pairs, haps, head_dim, 2 * LANES)
    q_row, state = pl.pallas_call(
        functools.partial(row_kernel, head_dim, places),
        grid=(haps,),
        in_specs=hap_specs + [once(query_row)] * 3,
        out_specs=[row_spec, state_spec],
        out_shape=[full_rows, jax.ShapeDtypeStruct(state_shape, BF16)],
        compiler_params=PARAMS,
        cost_estimate=cost(0),
        name="row",
    )(*normed, query_row, key_row, value_row)

    shares = state.reshape(m, -1, 2 * LANES)
    shares = lax.all_to_all(shares, "pos", split_axis=0, concat_axis=0, tiled=True)
    share = jnp.sum(shares.astype(F32), axis=0).astype(BF16)

    column_outs = None
    for c in range(chunks):
        blocks = [arrived[places[c, k][0]] for k in range(n)]
        extra = []
        if c > 0:
            blocks, _unused = lax.optimization_barrier((blocks, share))
            extra = [column_outs[places[0, 1][0]]] if n > 1 else []
        every = pltpu.VMEM((haps * n, depth, width), BF16)
        results = pl.pallas_call(
            functools.partial(column_kernel, head_dim, n),
            grid=(1,),
            in_specs=[whole(temper_flat)]
            + [once(query_col)] * 3
            + [piece_spec(c, k) for k in range(n)]
            + [anywhere] * len(extra),
            out_specs=[piece_spec(c, k) for k in range(n)],
            out_shape=[shapes[places[c, k][0]] for k in range(n)],
            scratch_shapes=[every] * 3,
            input_output_aliases={4 + n: 1} if extra else {},
            compiler_params=PARAMS,
            cost_estimate=cost(COLUMN_COSTS[c]),
            name="column",
        )(temper_flat, query_col, key_col, value_col, *blocks, *extra)
        if column_outs is None:
            column_outs = [None] * len(shapes)
        for k in range(n):
            column_outs[places[c, k][0]] = results[k]
    returned = send_all(column_outs)

    state = lax.all_gather(share, "pos", axis=0, tiled=True).reshape(state_shape)
    acc = pl.pallas_call(
        functools.partial(along_kernel, head_dim, order),
        grid=(haps,),
        in_specs=[SCALARS, rows_spec, row_spec, state_spec, whole(head_gain_flat), once(out_row)],
        out_specs=pl.BlockSpec((1, len(order), depth, width), lambda r: (r, 0, 0, 0)),
        out_shape=jax.ShapeDtypeStruct((haps, len(order), depth, width), F32),
        scratch_shapes=[pltpu.VMEM((length, width), BF16)],
        compiler_params=PARAMS,
        cost_estimate=cost(0),
        name="along",
    )(place, rows5, q_row, state, head_gain_flat, out_row)

    early = [(0, k) for k in range(n) if k != 1] if chunks > 1 else []
    late = [piece for piece in order if piece not in early]
    updated = None
    for pieces in [early, late] if early else [late]:
        extra = [] if updated is None else [updated]
        count = len(pieces)
        updated = pl.pallas_call(
            functools.partial(finish_kernel, pieces, order),
            grid=(1,),
            in_specs=[SCALARS, anywhere, once(out_col)]
            + [piece_spec(c, k) for c, k in pieces]
            + [anywhere] * len(extra),
            out_specs=anywhere,
            out_shape=jax.ShapeDtypeStruct(rows5.shape, BF16),
            scratch_shapes=[
                pltpu.VMEM((count, haps, depth, width), F32),
                pltpu.VMEM((count, haps, depth, width), BF16),
                pltpu.SemaphoreType.DMA((count,)),
                pltpu.SemaphoreType.DMA((count,)),
            ],
            input_output_aliases={3 + count: 0} if extra else {},
            compiler_params=PARAMS,
            cost_estimate=cost(FINISH_COSTS[0 if pieces is early else 1]),
            name="finish",
        )(place, acc, out_col, *[returned[places[c, k][0]] for c, k in pieces], *extra)
    return updated.reshape(haps, length, width)


def solution(mesh):
    sizes = (mesh.shape["hap"], mesh.shape["pos"])
    return jax.shard_map(
        functools.partial(local, sizes),
        mesh=mesh,
        in_specs=(P("hap", "pos", None), P(), P(), P(), P(), P(), P(), P(), P(), P(), P(), P()),
        out_specs=P("hap", "pos", None),
        check_vma=False,
    )
```

```python
import functools

import jax
import jax.numpy as jnp
from jax import lax
from jax.experimental import pallas as pl
from jax.experimental.pallas import tpu as pltpu
from jax.sharding import PartitionSpec as P

EPS = 1e-06
LANES = 128
TILE = 16
F32 = jnp.float32
BF16 = jnp.bfloat16
VMEM_MIB = 24
PACK_COST = 10
ROW_COST = 20
QUERY_COST = 5
SHARE_COST = 5
TIE_C1 = 'state'
ALONG_COST = 0
COLUMN_COSTS = (200, 30)
FINISH_COSTS = (30, 0)


def last_dims(left, right):
    return lax.dot_general(left, right, (((1,), (1,)), ((), ())), preferred_element_type=F32)


def first_dims(left, right):
    return lax.dot_general(left, right, (((0,), (0,)), ((), ())), preferred_element_type=F32)


def plain(left, right):
    return jnp.dot(left, right, preferred_element_type=F32)


def lane_of(shape):
    return lax.broadcasted_iota(jnp.int32, shape, len(shape) - 1)


def group_ones(size, head_dim):
    rows = lax.broadcasted_iota(jnp.int32, (size, size), 0) // head_dim
    cols = lax.broadcasted_iota(jnp.int32, (size, size), 1) // head_dim
    return jnp.where(rows == cols, 1.0, 0.0).astype(BF16)


def head_square_sums(values, ones):
    size = ones.shape[0]
    parts = []
    for start in range(0, values.shape[1], size):
        piece = values[:, start : start + size]
        square = piece * piece
        high = square.astype(BF16)
        low = (square - high.astype(F32)).astype(BF16)
        parts.append(plain(high, ones) + plain(low, ones))
    return jnp.concatenate(parts, axis=1) if len(parts) > 1 else parts[0]


def feature_pair(values):
    small = jnp.exp(-jnp.abs(values))
    up = values > 0
    plus = jnp.where(up, values + 1.0, small).astype(BF16)
    minus = jnp.where(up, small, 1.0 - values).astype(BF16)
    return plus, minus


def pack_kernel(head_dim, places, place_ref, temper_ref, rows_ref, gain_ref, *outs):
    z = place_ref[0]
    spread = outs[-1]
    for head in range(temper_ref.shape[0]):
        spread[:, head * head_dim : (head + 1) * head_dim] = jnp.full(
            (1, head_dim), temper_ref[head], F32
        )
    gain = gain_ref[...]
    for (c, k), (index, slot) in places.items():
        block = rows_ref[0, z ^ k, c].astype(F32)
        scale = lax.rsqrt(jnp.mean(block * block, axis=-1, keepdims=True) + EPS)
        outs[index][slot, 0] = (block * scale * gain).astype(BF16)


def share_kernel(shares_ref, out_ref):
    total = shares_ref[0].astype(F32)
    for i in range(1, shares_ref.shape[0]):
        total = total + shares_ref[i].astype(F32)
    out_ref[...] = total.astype(BF16)


def row_kernel(head_dim, places, *refs):
    wk_ref, wv_ref, state_ref = refs[-3:]
    rows = jnp.concatenate([refs[index][slot, 0] for index, slot in places.values()], axis=0)
    keys = plain(rows, wk_ref[...]).astype(BF16)
    values = plain(rows, wv_ref[...]).astype(BF16)
    first_head = lane_of((head_dim, 2 * LANES)) % LANES < head_dim
    for pair in range(keys.shape[1] // LANES):
        lower = pair * LANES
        plus, minus = feature_pair(keys[:, lower : lower + LANES].astype(F32))
        features = jnp.concatenate([plus, minus], axis=1)
        state = first_dims(values[:, lower : lower + LANES], features)
        folded = jnp.where(first_head, state[:head_dim], state[head_dim:])
        state_ref[pair, 0] = folded.astype(BF16)


def query_kernel(places, *refs):
    wq_ref, q_ref = refs[-2:]
    rows = jnp.concatenate([refs[index][slot, 0] for index, slot in places.values()], axis=0)
    q_ref[0] = plain(rows, wq_ref[...]).astype(BF16)


def along_kernel(head_dim, order, place_ref, rows_ref, q_ref, state_ref, gain_ref, wo_ref, out_ref, mixed):
    z = place_ref[0]
    first_head = lane_of((head_dim, 2 * LANES)) % LANES < head_dim
    ones = group_ones(2 * LANES, head_dim)
    alongs = []
    for pair in range(state_ref.shape[0]):
        lower = pair * LANES
        plus, minus = feature_pair(q_ref[0, :, lower : lower + LANES].astype(F32))
        features = jnp.concatenate([plus, minus], axis=1)
        folded = state_ref[pair, 0]
        none = jnp.zeros_like(folded)
        state = jnp.concatenate(
            [jnp.where(first_head, folded, none), jnp.where(first_head, none, folded)], axis=0
        )
        alongs.append(last_dims(features, state))
        if pair % 2 == 1:
            lower -= LANES
            wide = jnp.concatenate(alongs[-2:], axis=1)
            mean = head_square_sums(wide, ones) * (1.0 / head_dim)
            scaled = wide * lax.rsqrt(mean + EPS) * gain_ref[:, lower : lower + 2 * LANES]
            mixed[:, lower : lower + 2 * LANES] = scaled.astype(BF16)
    row_out = plain(mixed[...], wo_ref[...])
    depth = rows_ref.shape[3]
    for i, (c, k) in enumerate(order):
        out_ref[0, i] = rows_ref[0, z ^ k, c].astype(F32) + row_out[i * depth : (i + 1) * depth]


def column_kernel(head_dim, count, temper_ref, wq_ref, wk_ref, wv_ref, *refs):
    blocks = refs[:count]
    outs = refs[-3 - count : -3]
    q_all, k_all, v_all = refs[-3:]
    _one, haps, depth, width = blocks[0].shape
    rows = jnp.concatenate([block[0, r] for block in blocks for r in range(haps)], axis=0)
    shape = q_all.shape
    ones = group_ones(2 * LANES, head_dim)
    q = plain(rows, wq_ref[...]).astype(BF16).astype(F32)
    q = q * lax.rsqrt(head_square_sums(q, ones) + EPS) * temper_ref[...]
    q_all[...] = q.astype(BF16).reshape(shape)
    k = plain(rows, wk_ref[...]).astype(BF16).astype(F32)
    k = k * lax.rsqrt(head_square_sums(k, ones) + EPS)
    k_all[...] = k.astype(BF16).reshape(shape)
    v_all[...] = plain(rows, wv_ref[...]).astype(BF16).reshape(shape)
    all_haps = shape[0]
    many = all_haps * TILE
    same = (
        lax.broadcasted_iota(jnp.int32, (many, many), 0) % TILE
        == lax.broadcasted_iota(jnp.int32, (many, many), 1) % TILE
    )
    first_head = lane_of((many, LANES)) < head_dim
    none = jnp.zeros((many, LANES), BF16)
    one = jnp.ones((many, LANES), BF16)
    for start in range(0, depth, TILE):
        for lower in range(0, width, LANES):
            at = (slice(None), slice(start, start + TILE), slice(lower, lower + LANES))
            query = q_all[at].reshape(many, LANES)
            key = k_all[at].reshape(many, LANES)
            value = v_all[at].reshape(many, LANES)
            score_a = last_dims(jnp.where(first_head, query, none), key)
            score_b = last_dims(jnp.where(first_head, none, query), key)
            weight_a = jnp.where(same, jnp.exp(score_a), 0.0).astype(BF16)
            weight_b = jnp.where(same, jnp.exp(score_b), 0.0).astype(BF16)
            sum_a = plain(weight_a, jnp.where(first_head, value, one))
            sum_b = plain(weight_b, jnp.where(first_head, one, value))
            summed = jnp.where(first_head, sum_a, sum_b)
            total = pltpu.roll(jnp.where(first_head, sum_b, sum_a), head_dim, 1)
            result = (summed / total).astype(BF16).reshape(all_haps, TILE, LANES)
            for k in range(count):
                outs[k][0, :, start : start + TILE, lower : lower + LANES] = result[
                    k * haps : (k + 1) * haps
                ]


def finish_kernel(pieces, order, place_ref, acc_ref, wo_ref, *refs):
    mixed = refs[: len(pieces)]
    out_ref, acc, result, acc_sems, out_sems = refs[-5:]
    z = place_ref[0]
    _one, haps, depth, _width = mixed[0].shape
    loads = [
        pltpu.make_async_copy(acc_ref.at[:, order.index(piece)], acc.at[i], acc_sems.at[i])
        for i, piece in enumerate(pieces)
    ]
    for load in loads:
        load.start()
    flat = jnp.concatenate([block[0, r] for block in mixed for r in range(haps)], axis=0)
    col_out = plain(flat, wo_ref[...])
    stores = []
    for i, (c, k) in enumerate(pieces):
        loads[i].wait()
        for r in range(haps):
            lower = (i * haps + r) * depth
            result[i, r] = (acc[i, r] + col_out[lower : lower + depth]).astype(BF16)
        store = pltpu.make_async_copy(result.at[i], out_ref.at[:, z ^ k, c], out_sems.at[i])
        store.start()
        stores.append(store)
    for store in stores:
        store.wait()


def whole(array):
    zeros = (0,) * array.ndim
    return pl.BlockSpec(array.shape, lambda *_: zeros)


def once(array):
    zeros = (0,) * array.ndim
    return pl.BlockSpec(array.shape, lambda *_: zeros, pipeline_mode=pl.Buffered(1))


SCALARS = pl.BlockSpec(memory_space=pltpu.SMEM)
PARAMS = pltpu.CompilerParams(vmem_limit_bytes=VMEM_MIB * 1024 * 1024)


def cost(micros):
    return pl.CostEstimate(flops=int(micros * 1e9), bytes_accessed=1, transcendentals=0)


def local(
    sizes,
    haplo_rows,
    norm_gain,
    query_row,
    key_row,
    value_row,
    out_row,
    head_gain,
    query_col,
    key_col,
    value_col,
    out_col,
    temper,
):
    n, m = sizes
    haps, length, width = haplo_rows.shape
    heads = temper.shape[0]
    head_dim = width // heads
    owned = length // n
    chunks = 2 if owned % (2 * TILE) == 0 else 1
    depth = owned // chunks
    pairs = width // LANES
    place = lax.axis_index("hap").astype(jnp.int32)[None]
    rows5 = haplo_rows.reshape(haps, n, chunks, depth, width)
    gain_flat = norm_gain[None, :]
    head_gain_flat = head_gain[None, :]
    flat = jax.ShapeDtypeStruct((1, width), F32)
    anywhere = pl.BlockSpec(memory_space=pl.ANY)

    def exchange(array, k):
        return lax.ppermute(array, "hap", [(i, i ^ k) for i in range(n)])

    order = [(c, k) for c in range(chunks) for k in range(n)]
    places, lengths = {}, []
    for c, k in order:
        if k == 1 and c > 0:
            places[c, k] = (places[0, 1][0], c)
        else:
            places[c, k] = (len(lengths), 0)
            lengths.append(chunks if k == 1 else 1)
    shapes = [jax.ShapeDtypeStruct((many, haps, depth, width), BF16) for many in lengths]
    hap_specs = [
        pl.BlockSpec((many, 1, depth, width), lambda r: (0, r, 0, 0)) for many in lengths
    ]
    rows_spec = pl.BlockSpec((1, n, chunks, depth, width), lambda r: (r, 0, 0, 0, 0))

    def piece_spec(c, k):
        slot = places[c, k][1]
        return pl.BlockSpec((1, haps, depth, width), lambda *_: (slot, 0, 0, 0))

    *normed, temper_flat = pl.pallas_call(
        functools.partial(pack_kernel, head_dim, places),
        grid=(haps,),
        in_specs=[SCALARS, SCALARS, rows_spec, whole(gain_flat)],
        out_specs=hap_specs + [whole(flat)],
        out_shape=shapes + [flat],
        compiler_params=PARAMS,
        cost_estimate=cost(PACK_COST),
        name="pack",
    )(place, temper, rows5, gain_flat)

    def send_all(arrays):
        got = {}
        sent = list(arrays)
        for c, k in order[1:] if n > 1 else []:
            index, slot = places[c, k]
            if k > 0 and slot == 0:
                sent[index] = exchange(arrays[index], k)
        return sent

    full_rows = jax.ShapeDtypeStruct((haps, length, width), BF16)
    row_spec = pl.BlockSpec((1, length, width), lambda r: (r, 0, 0))
    state_spec = pl.BlockSpec((pairs, 1, head_dim, 2 * LANES), lambda r: (0, r, 0, 0))
    state_shape = (pairs, haps, head_dim, 2 * LANES)
    state = pl.pallas_call(
        functools.partial(row_kernel, head_dim, places),
        grid=(haps,),
        in_specs=hap_specs + [once(key_row)] * 2,
        out_specs=state_spec,
        out_shape=jax.ShapeDtypeStruct(state_shape, BF16),
        compiler_params=PARAMS,
        cost_estimate=cost(ROW_COST),
        name="row",
    )(*normed, key_row, value_row)

    q_row = pl.pallas_call(
        functools.partial(query_kernel, places),
        grid=(haps,),
        in_specs=hap_specs + [once(query_row)],
        out_specs=row_spec,
        out_shape=full_rows,
        compiler_params=PARAMS,
        cost_estimate=cost(QUERY_COST),
        name="query",
    )(*normed, query_row)

    waiting = [
        index for index in range(len(lengths)) if any(places[c, k][0] == index for c, k in order if c > 0 and k > 1)
    ]
    held, state = lax.optimization_barrier(([normed[index] for index in waiting], state))
    queue = list(normed)
    for index, array in zip(waiting, held):
        queue[index] = array
    arrived = send_all(queue)

    shares = state.reshape(m, -1, 2 * LANES)
    shares = lax.all_to_all(shares, "pos", split_axis=0, concat_axis=0, tiled=True)

    state = None

    def add_up(shares):
        share = pl.pallas_call(
            share_kernel,
            grid=(1,),
            in_specs=[whole(shares)],
            out_specs=pl.BlockSpec(shares.shape[1:], lambda *_: (0, 0)),
            out_shape=jax.ShapeDtypeStruct(shares.shape[1:], BF16),
            compiler_params=PARAMS,
            cost_estimate=cost(SHARE_COST),
            name="share",
        )(shares)
        return lax.all_gather(share, "pos", axis=0, tiled=True).reshape(state_shape)

    column_outs = None
    for c in range(chunks):
        blocks = [arrived[places[c, k][0]] for k in range(n)]
        extra = []
        if c == 0:
            blocks, q_row = lax.optimization_barrier((blocks, q_row))
        if c > 0:
            if TIE_C1 == "state":
                state = add_up(shares)
                blocks, state = lax.optimization_barrier((blocks, state))
            elif TIE_C1 == "shares":
                blocks, shares = lax.optimization_barrier((blocks, shares))
            extra = [column_outs[places[0, 1][0]]] if n > 1 else []
        every = pltpu.VMEM((haps * n, depth, width), BF16)
        results = pl.pallas_call(
            functools.partial(column_kernel, head_dim, n),
            grid=(1,),
            in_specs=[whole(temper_flat)]
            + [once(query_col)] * 3
            + [piece_spec(c, k) for k in range(n)]
            + [anywhere] * len(extra),
            out_specs=[piece_spec(c, k) for k in range(n)],
            out_shape=[shapes[places[c, k][0]] for k in range(n)],
            scratch_shapes=[every] * 3,
            input_output_aliases={4 + n: 1} if extra else {},
            compiler_params=PARAMS,
            cost_estimate=cost(COLUMN_COSTS[c]),
            name="column",
        )(temper_flat, query_col, key_col, value_col, *blocks, *extra)
        if column_outs is None:
            column_outs = [None] * len(shapes)
        for k in range(n):
            column_outs[places[c, k][0]] = results[k]
    returned = send_all(column_outs)

    if state is None:
        state = add_up(shares)
    acc = pl.pallas_call(
        functools.partial(along_kernel, head_dim, order),
        grid=(haps,),
        in_specs=[SCALARS, rows_spec, row_spec, state_spec, whole(head_gain_flat), once(out_row)],
        out_specs=pl.BlockSpec((1, len(order), depth, width), lambda r: (r, 0, 0, 0)),
        out_shape=jax.ShapeDtypeStruct((haps, len(order), depth, width), F32),
        scratch_shapes=[pltpu.VMEM((length, width), BF16)],
        compiler_params=PARAMS,
        cost_estimate=cost(ALONG_COST),
        name="along",
    )(place, rows5, q_row, state, head_gain_flat, out_row)

    early = [(0, k) for k in range(n) if k != 1] if chunks > 1 else []
    late = [piece for piece in order if piece not in early]
    updated = None
    for pieces in [early, late] if early else [late]:
        extra = [] if updated is None else [updated]
        count = len(pieces)
        updated = pl.pallas_call(
            functools.partial(finish_kernel, pieces, order),
            grid=(1,),
            in_specs=[SCALARS, anywhere, once(out_col)]
            + [piece_spec(c, k) for c, k in pieces]
            + [anywhere] * len(extra),
            out_specs=anywhere,
            out_shape=jax.ShapeDtypeStruct(rows5.shape, BF16),
            scratch_shapes=[
                pltpu.VMEM((count, haps, depth, width), F32),
                pltpu.VMEM((count, haps, depth, width), BF16),
                pltpu.SemaphoreType.DMA((count,)),
                pltpu.SemaphoreType.DMA((count,)),
            ],
            input_output_aliases={3 + count: 0} if extra else {},
            compiler_params=PARAMS,
            cost_estimate=cost(FINISH_COSTS[0 if pieces is early else 1]),
            name="finish",
        )(place, acc, out_col, *[returned[places[c, k][0]] for c, k in pieces], *extra)
    return updated.reshape(haps, length, width)


def solution(mesh):
    sizes = (mesh.shape["hap"], mesh.shape["pos"])
    return jax.shard_map(
        functools.partial(local, sizes),
        mesh=mesh,
        in_specs=(P("hap", "pos", None), P(), P(), P(), P(), P(), P(), P(), P(), P(), P(), P()),
        out_specs=P("hap", "pos", None),
        check_vma=False,
    )
```

```python
import functools

import jax
import jax.numpy as jnp
from jax import lax
from jax.experimental import pallas as pl
from jax.experimental.pallas import tpu as pltpu
from jax.sharding import PartitionSpec as P

EPS = 1e-06
LANES = 128
TILE = 16
F32 = jnp.float32
BF16 = jnp.bfloat16
VMEM_MIB = 24
PACK_COST = 10
ROW_COST = 20
SPREAD_COST = 5
RAW = True
SHARE_COST = 5
TIE_C1 = 'state'
ALONG_COST = 0
COLUMN_COSTS = (200, 30)
FINISH_COSTS = (30, 0)


def last_dims(left, right):
    return lax.dot_general(left, right, (((1,), (1,)), ((), ())), preferred_element_type=F32)


def first_dims(left, right):
    return lax.dot_general(left, right, (((0,), (0,)), ((), ())), preferred_element_type=F32)


def plain(left, right):
    return jnp.dot(left, right, preferred_element_type=F32)


def lane_of(shape):
    return lax.broadcasted_iota(jnp.int32, shape, len(shape) - 1)


def group_ones(size, head_dim):
    rows = lax.broadcasted_iota(jnp.int32, (size, size), 0) // head_dim
    cols = lax.broadcasted_iota(jnp.int32, (size, size), 1) // head_dim
    return jnp.where(rows == cols, 1.0, 0.0).astype(BF16)


def head_square_sums(values, ones):
    size = ones.shape[0]
    parts = []
    for start in range(0, values.shape[1], size):
        piece = values[:, start : start + size]
        square = piece * piece
        high = square.astype(BF16)
        low = (square - high.astype(F32)).astype(BF16)
        parts.append(plain(high, ones) + plain(low, ones))
    return jnp.concatenate(parts, axis=1) if len(parts) > 1 else parts[0]


def feature_pair(values):
    small = jnp.exp(-jnp.abs(values))
    up = values > 0
    plus = jnp.where(up, values + 1.0, small).astype(BF16)
    minus = jnp.where(up, small, 1.0 - values).astype(BF16)
    return plus, minus


def normalise(rows, gain):
    wide = rows.astype(F32)
    scale = lax.rsqrt(jnp.mean(wide * wide, axis=-1, keepdims=True) + EPS)
    return (wide * scale * gain).astype(BF16)


def spread_kernel(head_dim, temper_ref, out_ref):
    for head in range(temper_ref.shape[0]):
        out_ref[:, head * head_dim : (head + 1) * head_dim] = jnp.full(
            (1, head_dim), temper_ref[head], F32
        )


def pack_kernel(places, place_ref, rows_ref, gain_ref, *outs):
    z = place_ref[0]
    gain = gain_ref[...]
    for (c, k), (index, slot) in places.items():
        outs[index][slot, 0] = normalise(rows_ref[0, z ^ k, c], gain)


def share_kernel(shares_ref, out_ref):
    total = shares_ref[0].astype(F32)
    for i in range(1, shares_ref.shape[0]):
        total = total + shares_ref[i].astype(F32)
    out_ref[...] = total.astype(BF16)


def row_kernel(head_dim, places, *refs):
    wk_ref, wv_ref, state_ref = refs[-3:]
    rows = jnp.concatenate([refs[index][slot, 0] for index, slot in places.values()], axis=0)
    keys = plain(rows, wk_ref[...]).astype(BF16)
    values = plain(rows, wv_ref[...]).astype(BF16)
    first_head = lane_of((head_dim, 2 * LANES)) % LANES < head_dim
    for pair in range(keys.shape[1] // LANES):
        lower = pair * LANES
        plus, minus = feature_pair(keys[:, lower : lower + LANES].astype(F32))
        features = jnp.concatenate([plus, minus], axis=1)
        state = first_dims(values[:, lower : lower + LANES], features)
        folded = jnp.where(first_head, state[:head_dim], state[head_dim:])
        state_ref[pair, 0] = folded.astype(BF16)


def along_kernel(
    head_dim, order, place_ref, rows_ref, norm_ref, wq_ref, state_ref, gain_ref, wo_ref, out_ref, mixed
):
    z = place_ref[0]
    rows = jnp.concatenate([rows_ref[0, z ^ k, c] for c, k in order], axis=0)
    queries = plain(normalise(rows, norm_ref[...]), wq_ref[...]).astype(BF16)
    first_head = lane_of((head_dim, 2 * LANES)) % LANES < head_dim
    ones = group_ones(2 * LANES, head_dim)
    alongs = []
    for pair in range(state_ref.shape[0]):
        lower = pair * LANES
        plus, minus = feature_pair(queries[:, lower : lower + LANES].astype(F32))
        features = jnp.concatenate([plus, minus], axis=1)
        folded = state_ref[pair, 0]
        none = jnp.zeros_like(folded)
        state = jnp.concatenate(
            [jnp.where(first_head, folded, none), jnp.where(first_head, none, folded)], axis=0
        )
        alongs.append(last_dims(features, state))
        if pair % 2 == 1:
            lower -= LANES
            wide = jnp.concatenate(alongs[-2:], axis=1)
            mean = head_square_sums(wide, ones) * (1.0 / head_dim)
            scaled = wide * lax.rsqrt(mean + EPS) * gain_ref[:, lower : lower + 2 * LANES]
            mixed[:, lower : lower + 2 * LANES] = scaled.astype(BF16)
    row_out = plain(mixed[...], wo_ref[...])
    depth = rows_ref.shape[3]
    for i, (c, k) in enumerate(order):
        out_ref[0, i] = rows_ref[0, z ^ k, c].astype(F32) + row_out[i * depth : (i + 1) * depth]


def column_kernel(head_dim, raw, temper_ref, gain_ref, wq_ref, wk_ref, wv_ref, *refs):
    count = len(raw)
    blocks = refs[:count]
    outs = refs[-3 - count : -3]
    q_all, k_all, v_all = refs[-3:]
    _one, haps, depth, width = blocks[0].shape
    pieces = []
    for block, is_raw in zip(blocks, raw):
        piece = block[0].reshape(haps * depth, width)
        pieces.append(normalise(piece, gain_ref[...]) if is_raw else piece)
    rows = jnp.concatenate(pieces, axis=0)
    shape = q_all.shape
    ones = group_ones(2 * LANES, head_dim)
    q = plain(rows, wq_ref[...]).astype(BF16).astype(F32)
    q = q * lax.rsqrt(head_square_sums(q, ones) + EPS) * temper_ref[...]
    q_all[...] = q.astype(BF16).reshape(shape)
    k = plain(rows, wk_ref[...]).astype(BF16).astype(F32)
    k = k * lax.rsqrt(head_square_sums(k, ones) + EPS)
    k_all[...] = k.astype(BF16).reshape(shape)
    v_all[...] = plain(rows, wv_ref[...]).astype(BF16).reshape(shape)
    all_haps = shape[0]
    many = all_haps * TILE
    same = (
        lax.broadcasted_iota(jnp.int32, (2 * many, many), 0) % TILE
        == lax.broadcasted_iota(jnp.int32, (2 * many, many), 1) % TILE
    )
    first_head = lane_of((many, LANES)) < head_dim
    none = jnp.zeros((many, LANES), BF16)
    one = jnp.ones((many, LANES), BF16)
    for start in range(0, depth, TILE):
        for lower in range(0, width, LANES):
            at = (slice(None), slice(start, start + TILE), slice(lower, lower + LANES))
            query = q_all[at].reshape(many, LANES)
            key = k_all[at].reshape(many, LANES)
            value = v_all[at].reshape(many, LANES)
            queries = jnp.concatenate(
                [jnp.where(first_head, query, none), jnp.where(first_head, none, query)], axis=0
            )
            weight = jnp.where(same, jnp.exp(last_dims(queries, key)), 0.0).astype(BF16)
            sums = plain(weight, jnp.concatenate([value, one], axis=1))
            summed = jnp.where(first_head, sums[:many, :LANES], sums[many:, :LANES])
            total = jnp.where(first_head, sums[:many, LANES:], sums[many:, LANES:])
            result = (summed / total).astype(BF16).reshape(all_haps, TILE, LANES)
            for k in range(count):
                outs[k][0, :, start : start + TILE, lower : lower + LANES] = result[
                    k * haps : (k + 1) * haps
                ]


def finish_kernel(pieces, order, place_ref, acc_ref, wo_ref, *refs):
    mixed = refs[: len(pieces)]
    out_ref, acc, result, acc_sems, out_sems = refs[-5:]
    z = place_ref[0]
    _one, haps, depth, _width = mixed[0].shape
    loads = [
        pltpu.make_async_copy(acc_ref.at[:, order.index(piece)], acc.at[i], acc_sems.at[i])
        for i, piece in enumerate(pieces)
    ]
    for load in loads:
        load.start()
    flat = jnp.concatenate([block[0, r] for block in mixed for r in range(haps)], axis=0)
    col_out = plain(flat, wo_ref[...])
    stores = []
    for i, (c, k) in enumerate(pieces):
        loads[i].wait()
        for r in range(haps):
            lower = (i * haps + r) * depth
            result[i, r] = (acc[i, r] + col_out[lower : lower + depth]).astype(BF16)
        store = pltpu.make_async_copy(result.at[i], out_ref.at[:, z ^ k, c], out_sems.at[i])
        store.start()
        stores.append(store)
    for store in stores:
        store.wait()


def whole(array):
    zeros = (0,) * array.ndim
    return pl.BlockSpec(array.shape, lambda *_: zeros)


def once(array):
    zeros = (0,) * array.ndim
    return pl.BlockSpec(array.shape, lambda *_: zeros, pipeline_mode=pl.Buffered(1))


SCALARS = pl.BlockSpec(memory_space=pltpu.SMEM)
PARAMS = pltpu.CompilerParams(vmem_limit_bytes=VMEM_MIB * 1024 * 1024)


def cost(micros):
    return pl.CostEstimate(flops=int(micros * 1e9), bytes_accessed=1, transcendentals=0)


def local(
    sizes,
    haplo_rows,
    norm_gain,
    query_row,
    key_row,
    value_row,
    out_row,
    head_gain,
    query_col,
    key_col,
    value_col,
    out_col,
    temper,
):
    n, m = sizes
    haps, length, width = haplo_rows.shape
    heads = temper.shape[0]
    head_dim = width // heads
    owned = length // n
    chunks = 2 if owned % (2 * TILE) == 0 else 1
    depth = owned // chunks
    pairs = width // LANES
    place = lax.axis_index("hap").astype(jnp.int32)[None]
    rows5 = haplo_rows.reshape(haps, n, chunks, depth, width)
    gain_flat = norm_gain[None, :]
    head_gain_flat = head_gain[None, :]
    flat = jax.ShapeDtypeStruct((1, width), F32)
    anywhere = pl.BlockSpec(memory_space=pl.ANY)

    def exchange(array, k):
        return lax.ppermute(array, "hap", [(i, i ^ k) for i in range(n)])

    order = [(c, k) for c in range(chunks) for k in range(n)]
    places, lengths = {}, []
    for c, k in order:
        if k == 1 and c > 0:
            places[c, k] = (places[0, 1][0], c)
        else:
            places[c, k] = (len(lengths), 0)
            lengths.append(chunks if k == 1 else 1)
    shapes = [jax.ShapeDtypeStruct((many, haps, depth, width), BF16) for many in lengths]
    hap_specs = [
        pl.BlockSpec((many, 1, depth, width), lambda r: (0, r, 0, 0)) for many in lengths
    ]
    rows_spec = pl.BlockSpec((1, n, chunks, depth, width), lambda r: (r, 0, 0, 0, 0))

    def piece_spec(c, k):
        slot = places[c, k][1]
        return pl.BlockSpec((1, haps, depth, width), lambda *_: (slot, 0, 0, 0))

    normed = pl.pallas_call(
        functools.partial(pack_kernel, places),
        grid=(haps,),
        in_specs=[SCALARS, rows_spec, whole(gain_flat)],
        out_specs=hap_specs,
        out_shape=shapes,
        compiler_params=PARAMS,
        cost_estimate=cost(PACK_COST),
        name="pack",
    )(place, rows5, gain_flat)

    def send_all(arrays):
        got = {}
        sent = list(arrays)
        for c, k in order[1:] if n > 1 else []:
            index, slot = places[c, k]
            if k > 0 and slot == 0:
                sent[index] = exchange(arrays[index], k)
        return sent

    state_spec = pl.BlockSpec((pairs, 1, head_dim, 2 * LANES), lambda r: (0, r, 0, 0))
    state_shape = (pairs, haps, head_dim, 2 * LANES)
    state = pl.pallas_call(
        functools.partial(row_kernel, head_dim, places),
        grid=(haps,),
        in_specs=hap_specs + [once(key_row)] * 2,
        out_specs=state_spec,
        out_shape=jax.ShapeDtypeStruct(state_shape, BF16),
        compiler_params=PARAMS,
        cost_estimate=cost(ROW_COST),
        name="row",
    )(*normed, key_row, value_row)

    temper_flat = pl.pallas_call(
        functools.partial(spread_kernel, head_dim),
        grid=(1,),
        in_specs=[SCALARS],
        out_specs=whole(flat),
        out_shape=flat,
        compiler_params=PARAMS,
        cost_estimate=cost(SPREAD_COST),
        name="spread",
    )(temper)

    waiting = [
        index for index in range(len(lengths)) if any(places[c, k][0] == index for c, k in order if c > 0 and k > 1)
    ]
    held, state = lax.optimization_barrier(([normed[index] for index in waiting], state))
    queue = list(normed)
    for index, array in zip(waiting, held):
        queue[index] = array
    raw = [k > 1 and RAW for k in range(n)]
    for k in range(n):
        if raw[k]:
            queue[places[0, k][0]] = lax.dynamic_index_in_dim(
                rows5[:, :, 0], place[0] ^ k, 1, keepdims=False
            )[None]
    arrived = send_all(queue)

    shares = state.reshape(m, -1, 2 * LANES)
    shares = lax.all_to_all(shares, "pos", split_axis=0, concat_axis=0, tiled=True)

    state = None

    def add_up(shares):
        share = pl.pallas_call(
            share_kernel,
            grid=(1,),
            in_specs=[whole(shares)],
            out_specs=pl.BlockSpec(shares.shape[1:], lambda *_: (0, 0)),
            out_shape=jax.ShapeDtypeStruct(shares.shape[1:], BF16),
            compiler_params=PARAMS,
            cost_estimate=cost(SHARE_COST),
            name="share",
        )(shares)
        return lax.all_gather(share, "pos", axis=0, tiled=True).reshape(state_shape)

    column_outs = None
    for c in range(chunks):
        blocks = [arrived[places[c, k][0]] for k in range(n)]
        extra = []
        if c > 0:
            if TIE_C1 == "state":
                state = add_up(shares)
                blocks, state = lax.optimization_barrier((blocks, state))
            elif TIE_C1 == "shares":
                blocks, shares = lax.optimization_barrier((blocks, shares))
            extra = [column_outs[places[0, 1][0]]] if n > 1 else []
        every = pltpu.VMEM((haps * n, depth, width), BF16)
        results = pl.pallas_call(
            functools.partial(column_kernel, head_dim, raw if c == 0 else [False] * n),
            grid=(1,),
            in_specs=[whole(temper_flat), whole(gain_flat)]
            + [once(query_col)] * 3
            + [piece_spec(c, k) for k in range(n)]
            + [anywhere] * len(extra),
            out_specs=[piece_spec(c, k) for k in range(n)],
            out_shape=[shapes[places[c, k][0]] for k in range(n)],
            scratch_shapes=[every] * 3,
            input_output_aliases={5 + n: 1} if extra else {},
            compiler_params=PARAMS,
            cost_estimate=cost(COLUMN_COSTS[c]),
            name="column",
        )(temper_flat, gain_flat, query_col, key_col, value_col, *blocks, *extra)
        if column_outs is None:
            column_outs = [None] * len(shapes)
        for k in range(n):
            column_outs[places[c, k][0]] = results[k]
    returned = send_all(column_outs)

    if state is None:
        state = add_up(shares)
    acc = pl.pallas_call(
        functools.partial(along_kernel, head_dim, order),
        grid=(haps,),
        in_specs=[SCALARS, rows_spec, whole(gain_flat), once(query_row), state_spec, whole(head_gain_flat), once(out_row)],
        out_specs=pl.BlockSpec((1, len(order), depth, width), lambda r: (r, 0, 0, 0)),
        out_shape=jax.ShapeDtypeStruct((haps, len(order), depth, width), F32),
        scratch_shapes=[pltpu.VMEM((length, width), BF16)],
        compiler_params=PARAMS,
        cost_estimate=cost(ALONG_COST),
        name="along",
    )(place, rows5, gain_flat, query_row, state, head_gain_flat, out_row)

    early = [(0, k) for k in range(n) if k != 1] if chunks > 1 else []
    late = [piece for piece in order if piece not in early]
    updated = None
    for pieces in [early, late] if early else [late]:
        extra = [] if updated is None else [updated]
        count = len(pieces)
        updated = pl.pallas_call(
            functools.partial(finish_kernel, pieces, order),
            grid=(1,),
            in_specs=[SCALARS, anywhere, once(out_col)]
            + [piece_spec(c, k) for c, k in pieces]
            + [anywhere] * len(extra),
            out_specs=anywhere,
            out_shape=jax.ShapeDtypeStruct(rows5.shape, BF16),
            scratch_shapes=[
                pltpu.VMEM((count, haps, depth, width), F32),
                pltpu.VMEM((count, haps, depth, width), BF16),
                pltpu.SemaphoreType.DMA((count,)),
                pltpu.SemaphoreType.DMA((count,)),
            ],
            input_output_aliases={3 + count: 0} if extra else {},
            compiler_params=PARAMS,
            cost_estimate=cost(FINISH_COSTS[0 if pieces is early else 1]),
            name="finish",
        )(place, acc, out_col, *[returned[places[c, k][0]] for c, k in pieces], *extra)
    return updated.reshape(haps, length, width)


def solution(mesh):
    sizes = (mesh.shape["hap"], mesh.shape["pos"])
    return jax.shard_map(
        functools.partial(local, sizes),
        mesh=mesh,
        in_specs=(P("hap", "pos", None), P(), P(), P(), P(), P(), P(), P(), P(), P(), P(), P()),
        out_specs=P("hap", "pos", None),
        check_vma=False,
    )
```

```python
import functools

import jax
import jax.numpy as jnp
from jax import lax
from jax.experimental import pallas as pl
from jax.experimental.pallas import tpu as pltpu
from jax.sharding import PartitionSpec as P

EPS = 1e-06
LANES = 128
TILE = 16
F32 = jnp.float32
BF16 = jnp.bfloat16
VMEM_MIB = 24
PACK_COST = 10
ROW_COST = 20
SPREAD_COST = 5
RAW = True
SHARE_COST = 5
TIE_C1 = 'state'
TIE_BACK = True
ALONG_COST = 0
COLUMN_COSTS = (200, 30)
FINISH_COSTS = (30, 0, 0)


def last_dims(left, right):
    return lax.dot_general(left, right, (((1,), (1,)), ((), ())), preferred_element_type=F32)


def first_dims(left, right):
    return lax.dot_general(left, right, (((0,), (0,)), ((), ())), preferred_element_type=F32)


def plain(left, right):
    return jnp.dot(left, right, preferred_element_type=F32)


def lane_of(shape):
    return lax.broadcasted_iota(jnp.int32, shape, len(shape) - 1)


def group_ones(size, head_dim):
    rows = lax.broadcasted_iota(jnp.int32, (size, size), 0) // head_dim
    cols = lax.broadcasted_iota(jnp.int32, (size, size), 1) // head_dim
    return jnp.where(rows == cols, 1.0, 0.0).astype(BF16)


def head_square_sums(values, ones):
    size = ones.shape[0]
    parts = []
    for start in range(0, values.shape[1], size):
        piece = values[:, start : start + size]
        square = piece * piece
        high = square.astype(BF16)
        low = (square - high.astype(F32)).astype(BF16)
        parts.append(plain(high, ones) + plain(low, ones))
    return jnp.concatenate(parts, axis=1) if len(parts) > 1 else parts[0]


def feature_pair(values):
    small = jnp.exp(-jnp.abs(values))
    up = values > 0
    plus = jnp.where(up, values + 1.0, small).astype(BF16)
    minus = jnp.where(up, small, 1.0 - values).astype(BF16)
    return plus, minus


def normalise(rows, gain):
    wide = rows.astype(F32)
    scale = lax.rsqrt(jnp.mean(wide * wide, axis=-1, keepdims=True) + EPS)
    return (wide * scale * gain).astype(BF16)


def spread_kernel(head_dim, temper_ref, out_ref):
    for head in range(temper_ref.shape[0]):
        out_ref[:, head * head_dim : (head + 1) * head_dim] = jnp.full(
            (1, head_dim), temper_ref[head], F32
        )


def pack_kernel(places, place_ref, rows_ref, gain_ref, *outs):
    z = place_ref[0]
    gain = gain_ref[...]
    for (c, k), (index, slot) in places.items():
        outs[index][slot, 0] = normalise(rows_ref[0, z ^ k, c], gain)


def share_kernel(shares_ref, out_ref):
    total = shares_ref[0].astype(F32)
    for i in range(1, shares_ref.shape[0]):
        total = total + shares_ref[i].astype(F32)
    out_ref[...] = total.astype(BF16)


def row_kernel(head_dim, places, *refs):
    wk_ref, wv_ref, state_ref = refs[-3:]
    rows = jnp.concatenate([refs[index][slot, 0] for index, slot in places.values()], axis=0)
    keys = plain(rows, wk_ref[...]).astype(BF16)
    values = plain(rows, wv_ref[...]).astype(BF16)
    first_head = lane_of((head_dim, 2 * LANES)) % LANES < head_dim
    for pair in range(keys.shape[1] // LANES):
        lower = pair * LANES
        plus, minus = feature_pair(keys[:, lower : lower + LANES].astype(F32))
        features = jnp.concatenate([plus, minus], axis=1)
        state = first_dims(values[:, lower : lower + LANES], features)
        folded = jnp.where(first_head, state[:head_dim], state[head_dim:])
        state_ref[pair, 0] = folded.astype(BF16)


def along_kernel(
    head_dim, order, place_ref, rows_ref, norm_ref, wq_ref, state_ref, gain_ref, wo_ref, out_ref, mixed
):
    z = place_ref[0]
    rows = jnp.concatenate([rows_ref[0, z ^ k, c] for c, k in order], axis=0)
    queries = plain(normalise(rows, norm_ref[...]), wq_ref[...]).astype(BF16)
    first_head = lane_of((head_dim, 2 * LANES)) % LANES < head_dim
    ones = group_ones(2 * LANES, head_dim)
    alongs = []
    for pair in range(state_ref.shape[0]):
        lower = pair * LANES
        plus, minus = feature_pair(queries[:, lower : lower + LANES].astype(F32))
        features = jnp.concatenate([plus, minus], axis=1)
        folded = state_ref[pair, 0]
        none = jnp.zeros_like(folded)
        state = jnp.concatenate(
            [jnp.where(first_head, folded, none), jnp.where(first_head, none, folded)], axis=0
        )
        alongs.append(last_dims(features, state))
        if pair % 2 == 1:
            lower -= LANES
            wide = jnp.concatenate(alongs[-2:], axis=1)
            mean = head_square_sums(wide, ones) * (1.0 / head_dim)
            scaled = wide * lax.rsqrt(mean + EPS) * gain_ref[:, lower : lower + 2 * LANES]
            mixed[:, lower : lower + 2 * LANES] = scaled.astype(BF16)
    row_out = plain(mixed[...], wo_ref[...])
    depth = rows_ref.shape[3]
    for i, (c, k) in enumerate(order):
        out_ref[0, i] = rows_ref[0, z ^ k, c].astype(F32) + row_out[i * depth : (i + 1) * depth]


def column_kernel(head_dim, raw, temper_ref, gain_ref, wq_ref, wk_ref, wv_ref, *refs):
    count = len(raw)
    blocks = refs[:count]
    outs = refs[-3 - count : -3]
    q_all, k_all, v_all = refs[-3:]
    _one, haps, depth, width = blocks[0].shape
    pieces = []
    for block, is_raw in zip(blocks, raw):
        piece = block[0].reshape(haps * depth, width)
        pieces.append(normalise(piece, gain_ref[...]) if is_raw else piece)
    rows = jnp.concatenate(pieces, axis=0)
    shape = q_all.shape
    ones = group_ones(2 * LANES, head_dim)
    q = plain(rows, wq_ref[...]).astype(BF16).astype(F32)
    q = q * lax.rsqrt(head_square_sums(q, ones) + EPS) * temper_ref[...]
    q_all[...] = q.astype(BF16).reshape(shape)
    k = plain(rows, wk_ref[...]).astype(BF16).astype(F32)
    k = k * lax.rsqrt(head_square_sums(k, ones) + EPS)
    k_all[...] = k.astype(BF16).reshape(shape)
    v_all[...] = plain(rows, wv_ref[...]).astype(BF16).reshape(shape)
    all_haps = shape[0]
    many = all_haps * TILE
    same = (
        lax.broadcasted_iota(jnp.int32, (2 * many, many), 0) % TILE
        == lax.broadcasted_iota(jnp.int32, (2 * many, many), 1) % TILE
    )
    first_head = lane_of((many, LANES)) < head_dim
    none = jnp.zeros((many, LANES), BF16)
    one = jnp.ones((many, LANES), BF16)
    for start in range(0, depth, TILE):
        for lower in range(0, width, LANES):
            at = (slice(None), slice(start, start + TILE), slice(lower, lower + LANES))
            query = q_all[at].reshape(many, LANES)
            key = k_all[at].reshape(many, LANES)
            value = v_all[at].reshape(many, LANES)
            queries = jnp.concatenate(
                [jnp.where(first_head, query, none), jnp.where(first_head, none, query)], axis=0
            )
            weight = jnp.where(same, jnp.exp(last_dims(queries, key)), 0.0).astype(BF16)
            sums = plain(weight, jnp.concatenate([value, one], axis=1))
            summed = jnp.where(first_head, sums[:many, :LANES], sums[many:, :LANES])
            total = jnp.where(first_head, sums[:many, LANES:], sums[many:, LANES:])
            result = (summed / total).astype(BF16).reshape(all_haps, TILE, LANES)
            for k in range(count):
                outs[k][0, :, start : start + TILE, lower : lower + LANES] = result[
                    k * haps : (k + 1) * haps
                ]


def finish_kernel(pieces, order, place_ref, acc_ref, wo_ref, *refs):
    mixed = refs[: len(pieces)]
    out_ref, acc, result, acc_sems, out_sems = refs[-5:]
    z = place_ref[0]
    _one, haps, depth, _width = mixed[0].shape
    loads = [
        pltpu.make_async_copy(acc_ref.at[:, order.index(piece)], acc.at[i], acc_sems.at[i])
        for i, piece in enumerate(pieces)
    ]
    for load in loads:
        load.start()
    flat = jnp.concatenate([block[0, r] for block in mixed for r in range(haps)], axis=0)
    col_out = plain(flat, wo_ref[...])
    stores = []
    for i, (c, k) in enumerate(pieces):
        loads[i].wait()
        for r in range(haps):
            lower = (i * haps + r) * depth
            result[i, r] = (acc[i, r] + col_out[lower : lower + depth]).astype(BF16)
        store = pltpu.make_async_copy(result.at[i], out_ref.at[:, z ^ k, c], out_sems.at[i])
        store.start()
        stores.append(store)
    for store in stores:
        store.wait()


def whole(array):
    zeros = (0,) * array.ndim
    return pl.BlockSpec(array.shape, lambda *_: zeros)


def once(array):
    zeros = (0,) * array.ndim
    return pl.BlockSpec(array.shape, lambda *_: zeros, pipeline_mode=pl.Buffered(1))


SCALARS = pl.BlockSpec(memory_space=pltpu.SMEM)
PARAMS = pltpu.CompilerParams(vmem_limit_bytes=VMEM_MIB * 1024 * 1024)


def cost(micros):
    return pl.CostEstimate(flops=int(micros * 1e9), bytes_accessed=1, transcendentals=0)


def local(
    sizes,
    haplo_rows,
    norm_gain,
    query_row,
    key_row,
    value_row,
    out_row,
    head_gain,
    query_col,
    key_col,
    value_col,
    out_col,
    temper,
):
    n, m = sizes
    haps, length, width = haplo_rows.shape
    heads = temper.shape[0]
    head_dim = width // heads
    owned = length // n
    chunks = 2 if owned % (2 * TILE) == 0 else 1
    depth = owned // chunks
    pairs = width // LANES
    place = lax.axis_index("hap").astype(jnp.int32)[None]
    rows5 = haplo_rows.reshape(haps, n, chunks, depth, width)
    gain_flat = norm_gain[None, :]
    head_gain_flat = head_gain[None, :]
    flat = jax.ShapeDtypeStruct((1, width), F32)
    anywhere = pl.BlockSpec(memory_space=pl.ANY)

    def exchange(array, k):
        return lax.ppermute(array, "hap", [(i, i ^ k) for i in range(n)])

    order = [(c, k) for c in range(chunks) for k in range(n)]
    places, lengths = {}, []
    for c, k in order:
        if k == 1 and c > 0:
            places[c, k] = (places[0, 1][0], c)
        else:
            places[c, k] = (len(lengths), 0)
            lengths.append(chunks if k == 1 else 1)
    shapes = [jax.ShapeDtypeStruct((many, haps, depth, width), BF16) for many in lengths]
    hap_specs = [
        pl.BlockSpec((many, 1, depth, width), lambda r: (0, r, 0, 0)) for many in lengths
    ]
    rows_spec = pl.BlockSpec((1, n, chunks, depth, width), lambda r: (r, 0, 0, 0, 0))

    def piece_spec(c, k):
        slot = places[c, k][1]
        return pl.BlockSpec((1, haps, depth, width), lambda *_: (slot, 0, 0, 0))

    normed = pl.pallas_call(
        functools.partial(pack_kernel, places),
        grid=(haps,),
        in_specs=[SCALARS, rows_spec, whole(gain_flat)],
        out_specs=hap_specs,
        out_shape=shapes,
        compiler_params=PARAMS,
        cost_estimate=cost(PACK_COST),
        name="pack",
    )(place, rows5, gain_flat)

    def send_all(arrays):
        got = {}
        sent = list(arrays)
        for c, k in order[1:] if n > 1 else []:
            index, slot = places[c, k]
            if k > 0 and slot == 0:
                sent[index] = exchange(arrays[index], k)
        return sent

    state_spec = pl.BlockSpec((pairs, 1, head_dim, 2 * LANES), lambda r: (0, r, 0, 0))
    state_shape = (pairs, haps, head_dim, 2 * LANES)
    state = pl.pallas_call(
        functools.partial(row_kernel, head_dim, places),
        grid=(haps,),
        in_specs=hap_specs + [once(key_row)] * 2,
        out_specs=state_spec,
        out_shape=jax.ShapeDtypeStruct(state_shape, BF16),
        compiler_params=PARAMS,
        cost_estimate=cost(ROW_COST),
        name="row",
    )(*normed, key_row, value_row)

    temper_flat = pl.pallas_call(
        functools.partial(spread_kernel, head_dim),
        grid=(1,),
        in_specs=[SCALARS],
        out_specs=whole(flat),
        out_shape=flat,
        compiler_params=PARAMS,
        cost_estimate=cost(SPREAD_COST),
        name="spread",
    )(temper)

    waiting = [
        index for index in range(len(lengths)) if any(places[c, k][0] == index for c, k in order if c > 0 and k > 1)
    ]
    held, state = lax.optimization_barrier(([normed[index] for index in waiting], state))
    queue = list(normed)
    for index, array in zip(waiting, held):
        queue[index] = array
    raw = [k > 1 and RAW for k in range(n)]
    for k in range(n):
        if raw[k]:
            queue[places[0, k][0]] = lax.dynamic_index_in_dim(
                rows5[:, :, 0], place[0] ^ k, 1, keepdims=False
            )[None]
    arrived = send_all(queue)

    shares = state.reshape(m, -1, 2 * LANES)
    shares = lax.all_to_all(shares, "pos", split_axis=0, concat_axis=0, tiled=True)

    state = None

    def add_up(shares):
        share = pl.pallas_call(
            share_kernel,
            grid=(1,),
            in_specs=[whole(shares)],
            out_specs=pl.BlockSpec(shares.shape[1:], lambda *_: (0, 0)),
            out_shape=jax.ShapeDtypeStruct(shares.shape[1:], BF16),
            compiler_params=PARAMS,
            cost_estimate=cost(SHARE_COST),
            name="share",
        )(shares)
        return lax.all_gather(share, "pos", axis=0, tiled=True).reshape(state_shape)

    one_piece = jax.ShapeDtypeStruct((1, haps, depth, width), BF16)
    one_spec = pl.BlockSpec(one_piece.shape, lambda *_: (0, 0, 0, 0))
    returned = {}
    for c in range(chunks):
        blocks = [arrived[places[c, k][0]] for k in range(n)]
        if c > 0:
            if TIE_C1 == "state":
                state = add_up(shares)
                blocks, state = lax.optimization_barrier((blocks, state))
            elif TIE_C1 == "shares":
                blocks, shares = lax.optimization_barrier((blocks, shares))
        every = pltpu.VMEM((haps * n, depth, width), BF16)
        results = pl.pallas_call(
            functools.partial(column_kernel, head_dim, raw if c == 0 else [False] * n),
            grid=(1,),
            in_specs=[whole(temper_flat), whole(gain_flat)]
            + [once(query_col)] * 3
            + [piece_spec(c, k) for k in range(n)],
            out_specs=[one_spec] * n,
            out_shape=[one_piece] * n,
            scratch_shapes=[every] * 3,
            compiler_params=PARAMS,
            cost_estimate=cost(COLUMN_COSTS[c]),
            name="column",
        )(temper_flat, gain_flat, query_col, key_col, value_col, *blocks)
        if TIE_BACK and c > 0 and n > 1:
            results, returned[0, 1] = lax.optimization_barrier((results, returned[0, 1]))
        for k in range(n):
            returned[c, k] = exchange(results[k], k) if k > 0 else results[k]

    if state is None:
        state = add_up(shares)
    acc = pl.pallas_call(
        functools.partial(along_kernel, head_dim, order),
        grid=(haps,),
        in_specs=[SCALARS, rows_spec, whole(gain_flat), once(query_row), state_spec, whole(head_gain_flat), once(out_row)],
        out_specs=pl.BlockSpec((1, len(order), depth, width), lambda r: (r, 0, 0, 0)),
        out_shape=jax.ShapeDtypeStruct((haps, len(order), depth, width), F32),
        scratch_shapes=[pltpu.VMEM((length, width), BF16)],
        compiler_params=PARAMS,
        cost_estimate=cost(ALONG_COST),
        name="along",
    )(place, rows5, gain_flat, query_row, state, head_gain_flat, out_row)

    groups = [[], [], []]
    for c, k in order:
        groups[2 if c == chunks - 1 and k > 1 else 0 if c == 0 and chunks > 1 else 1].append((c, k))
    updated = None
    for pieces, weight in zip(groups, FINISH_COSTS):
        if not pieces:
            continue
        extra = [] if updated is None else [updated]
        count = len(pieces)
        updated = pl.pallas_call(
            functools.partial(finish_kernel, pieces, order),
            grid=(1,),
            in_specs=[SCALARS, anywhere, once(out_col)]
            + [one_spec] * count
            + [anywhere] * len(extra),
            out_specs=anywhere,
            out_shape=jax.ShapeDtypeStruct(rows5.shape, BF16),
            scratch_shapes=[
                pltpu.VMEM((count, haps, depth, width), F32),
                pltpu.VMEM((count, haps, depth, width), BF16),
                pltpu.SemaphoreType.DMA((count,)),
                pltpu.SemaphoreType.DMA((count,)),
            ],
            input_output_aliases={3 + count: 0} if extra else {},
            compiler_params=PARAMS,
            cost_estimate=cost(weight),
            name="finish",
        )(place, acc, out_col, *[returned[piece] for piece in pieces], *extra)
    return updated.reshape(haps, length, width)


def solution(mesh):
    sizes = (mesh.shape["hap"], mesh.shape["pos"])
    return jax.shard_map(
        functools.partial(local, sizes),
        mesh=mesh,
        in_specs=(P("hap", "pos", None), P(), P(), P(), P(), P(), P(), P(), P(), P(), P(), P()),
        out_specs=P("hap", "pos", None),
        check_vma=False,
    )
```

```python
import functools

import jax
import jax.numpy as jnp
from jax import lax
from jax.experimental import pallas as pl
from jax.experimental.pallas import tpu as pltpu
from jax.sharding import PartitionSpec as P

EPS = 1e-06
LANES = 128
TILE = 16
F32 = jnp.float32
BF16 = jnp.bfloat16
VMEM_MIB = 24
PACK_COST = 10
ROW_COST = 20
SPREAD_COST = 5
SHARE_COST = 5
ALONG_COST = 0
COLUMN_COSTS = (200, 30)
FINISH_COSTS = (30, 0, 0)


def last_dims(left, right):
    return lax.dot_general(left, right, (((1,), (1,)), ((), ())), preferred_element_type=F32)


def first_dims(left, right):
    return lax.dot_general(left, right, (((0,), (0,)), ((), ())), preferred_element_type=F32)


def plain(left, right):
    return jnp.dot(left, right, preferred_element_type=F32)


def lane_of(shape):
    return lax.broadcasted_iota(jnp.int32, shape, len(shape) - 1)


def group_ones(size, head_dim):
    rows = lax.broadcasted_iota(jnp.int32, (size, size), 0) // head_dim
    cols = lax.broadcasted_iota(jnp.int32, (size, size), 1) // head_dim
    return jnp.where(rows == cols, 1.0, 0.0).astype(BF16)


def head_square_sums(values, ones):
    size = ones.shape[0]
    parts = []
    for start in range(0, values.shape[1], size):
        piece = values[:, start : start + size]
        square = piece * piece
        high = square.astype(BF16)
        low = (square - high.astype(F32)).astype(BF16)
        parts.append(plain(high, ones) + plain(low, ones))
    return jnp.concatenate(parts, axis=1) if len(parts) > 1 else parts[0]


def feature_pair(values):
    small = jnp.exp(-jnp.abs(values))
    up = values > 0
    plus = jnp.where(up, values + 1.0, small).astype(BF16)
    minus = jnp.where(up, small, 1.0 - values).astype(BF16)
    return plus, minus


def normalise(rows, gain):
    wide = rows.astype(F32)
    scale = lax.rsqrt(jnp.mean(wide * wide, axis=-1, keepdims=True) + EPS)
    return (wide * scale * gain).astype(BF16)


def spread_kernel(head_dim, temper_ref, out_ref):
    for head in range(temper_ref.shape[0]):
        out_ref[:, head * head_dim : (head + 1) * head_dim] = jnp.full(
            (1, head_dim), temper_ref[head], F32
        )


def pack_kernel(places, place_ref, rows_ref, gain_ref, *outs):
    z = place_ref[0]
    gain = gain_ref[...]
    for (c, k), (index, slot) in places.items():
        for r in range(rows_ref.shape[0]):
            outs[index][slot, r] = normalise(rows_ref[r, z ^ k, c], gain)


def share_kernel(shares_ref, out_ref):
    total = shares_ref[0].astype(F32)
    for i in range(1, shares_ref.shape[0]):
        total = total + shares_ref[i].astype(F32)
    out_ref[...] = total.astype(BF16)


def row_kernel(head_dim, places, *refs):
    wk_ref, wv_ref, state_ref = refs[-3:]
    haps = state_ref.shape[1]
    rows = jnp.concatenate(
        [refs[index][slot, r] for r in range(haps) for index, slot in places.values()], axis=0
    )
    length = rows.shape[0] // haps
    keys = plain(rows, wk_ref[...]).astype(BF16)
    values = plain(rows, wv_ref[...]).astype(BF16)
    first_head = lane_of((head_dim, 2 * LANES)) % LANES < head_dim
    for r in range(haps):
        here = slice(r * length, (r + 1) * length)
        for pair in range(keys.shape[1] // LANES):
            lanes = slice(pair * LANES, (pair + 1) * LANES)
            plus, minus = feature_pair(keys[here, lanes].astype(F32))
            features = jnp.concatenate([plus, minus], axis=1)
            state = first_dims(values[here, lanes], features)
            folded = jnp.where(first_head, state[:head_dim], state[head_dim:])
            state_ref[pair, r] = folded.astype(BF16)


def along_kernel(
    head_dim, order, place_ref, rows_ref, norm_ref, wq_ref, state_ref, gain_ref, wo_ref, out_ref, mixed
):
    z = place_ref[0]
    rows = jnp.concatenate([rows_ref[0, z ^ k, c] for c, k in order], axis=0)
    queries = plain(normalise(rows, norm_ref[...]), wq_ref[...]).astype(BF16)
    first_head = lane_of((head_dim, 2 * LANES)) % LANES < head_dim
    ones = group_ones(2 * LANES, head_dim)
    alongs = []
    for pair in range(state_ref.shape[0]):
        lower = pair * LANES
        plus, minus = feature_pair(queries[:, lower : lower + LANES].astype(F32))
        features = jnp.concatenate([plus, minus], axis=1)
        folded = state_ref[pair, 0]
        none = jnp.zeros_like(folded)
        state = jnp.concatenate(
            [jnp.where(first_head, folded, none), jnp.where(first_head, none, folded)], axis=0
        )
        alongs.append(last_dims(features, state))
        if pair % 2 == 1:
            lower -= LANES
            wide = jnp.concatenate(alongs[-2:], axis=1)
            mean = head_square_sums(wide, ones) * (1.0 / head_dim)
            scaled = wide * lax.rsqrt(mean + EPS) * gain_ref[:, lower : lower + 2 * LANES]
            mixed[:, lower : lower + 2 * LANES] = scaled.astype(BF16)
    row_out = plain(mixed[...], wo_ref[...])
    depth = rows_ref.shape[3]
    for i, (c, k) in enumerate(order):
        out_ref[0, i] = rows_ref[0, z ^ k, c].astype(F32) + row_out[i * depth : (i + 1) * depth]


def column_kernel(head_dim, raw, temper_ref, gain_ref, wq_ref, wk_ref, wv_ref, *refs):
    count = len(raw)
    blocks = refs[:count]
    outs = refs[-3 - count : -3]
    q_all, k_all, v_all = refs[-3:]
    _one, haps, depth, width = blocks[0].shape
    pieces = []
    for block, is_raw in zip(blocks, raw):
        piece = block[0].reshape(haps * depth, width)
        pieces.append(normalise(piece, gain_ref[...]) if is_raw else piece)
    rows = jnp.concatenate(pieces, axis=0)
    shape = q_all.shape
    ones = group_ones(2 * LANES, head_dim)
    q = plain(rows, wq_ref[...]).astype(BF16).astype(F32)
    q = q * lax.rsqrt(head_square_sums(q, ones) + EPS) * temper_ref[...]
    q_all[...] = q.astype(BF16).reshape(shape)
    k = plain(rows, wk_ref[...]).astype(BF16).astype(F32)
    k = k * lax.rsqrt(head_square_sums(k, ones) + EPS)
    k_all[...] = k.astype(BF16).reshape(shape)
    v_all[...] = plain(rows, wv_ref[...]).astype(BF16).reshape(shape)
    all_haps = shape[0]
    many = all_haps * TILE
    same = (
        lax.broadcasted_iota(jnp.int32, (2 * many, many), 0) % TILE
        == lax.broadcasted_iota(jnp.int32, (2 * many, many), 1) % TILE
    )
    first_head = lane_of((many, LANES)) < head_dim
    none = jnp.zeros((many, LANES), BF16)
    one = jnp.ones((many, LANES), BF16)
    for start in range(0, depth, TILE):
        for lower in range(0, width, LANES):
            at = (slice(None), slice(start, start + TILE), slice(lower, lower + LANES))
            query = q_all[at].reshape(many, LANES)
            key = k_all[at].reshape(many, LANES)
            value = v_all[at].reshape(many, LANES)
            queries = jnp.concatenate(
                [jnp.where(first_head, query, none), jnp.where(first_head, none, query)], axis=0
            )
            weight = jnp.where(same, jnp.exp(last_dims(queries, key)), 0.0).astype(BF16)
            sums = plain(weight, jnp.concatenate([value, one], axis=1))
            summed = jnp.where(first_head, sums[:many, :LANES], sums[many:, :LANES])
            total = jnp.where(first_head, sums[:many, LANES:], sums[many:, LANES:])
            result = (summed / total).astype(BF16).reshape(all_haps, TILE, LANES)
            for k in range(count):
                outs[k][0, :, start : start + TILE, lower : lower + LANES] = result[
                    k * haps : (k + 1) * haps
                ]


def finish_kernel(pieces, order, place_ref, acc_ref, wo_ref, *refs):
    mixed = refs[: len(pieces)]
    out_ref, acc, result, acc_sems, out_sems = refs[-5:]
    z = place_ref[0]
    _one, haps, depth, _width = mixed[0].shape
    loads = [
        pltpu.make_async_copy(acc_ref.at[:, order.index(piece)], acc.at[i], acc_sems.at[i])
        for i, piece in enumerate(pieces)
    ]
    for load in loads:
        load.start()
    flat = jnp.concatenate([block[0, r] for block in mixed for r in range(haps)], axis=0)
    col_out = plain(flat, wo_ref[...])
    stores = []
    for i, (c, k) in enumerate(pieces):
        loads[i].wait()
        for r in range(haps):
            lower = (i * haps + r) * depth
            result[i, r] = (acc[i, r] + col_out[lower : lower + depth]).astype(BF16)
        store = pltpu.make_async_copy(result.at[i], out_ref.at[:, z ^ k, c], out_sems.at[i])
        store.start()
        stores.append(store)
    for store in stores:
        store.wait()


def whole(array):
    zeros = (0,) * array.ndim
    return pl.BlockSpec(array.shape, lambda *_: zeros)


def once(array):
    zeros = (0,) * array.ndim
    return pl.BlockSpec(array.shape, lambda *_: zeros, pipeline_mode=pl.Buffered(1))


SCALARS = pl.BlockSpec(memory_space=pltpu.SMEM)
PARAMS = pltpu.CompilerParams(vmem_limit_bytes=VMEM_MIB * 1024 * 1024)


def cost(micros):
    return pl.CostEstimate(flops=int(micros * 1e9), bytes_accessed=1, transcendentals=0)


def local(
    sizes,
    haplo_rows,
    norm_gain,
    query_row,
    key_row,
    value_row,
    out_row,
    head_gain,
    query_col,
    key_col,
    value_col,
    out_col,
    temper,
):
    n, m = sizes
    haps, length, width = haplo_rows.shape
    heads = temper.shape[0]
    head_dim = width // heads
    owned = length // n
    chunks = 2 if owned % (2 * TILE) == 0 else 1
    depth = owned // chunks
    pairs = width // LANES
    place = lax.axis_index("hap").astype(jnp.int32)[None]
    rows5 = haplo_rows.reshape(haps, n, chunks, depth, width)
    gain_flat = norm_gain[None, :]
    head_gain_flat = head_gain[None, :]
    flat = jax.ShapeDtypeStruct((1, width), F32)
    anywhere = pl.BlockSpec(memory_space=pl.ANY)

    def exchange(array, k):
        return lax.ppermute(array, "hap", [(i, i ^ k) for i in range(n)])

    order = [(c, k) for c in range(chunks) for k in range(n)]
    places, lengths = {}, []
    for c, k in order:
        if k == 1 and c > 0:
            places[c, k] = (places[0, 1][0], c)
        else:
            places[c, k] = (len(lengths), 0)
            lengths.append(chunks if k == 1 else 1)
    shapes = [jax.ShapeDtypeStruct((many, haps, depth, width), BF16) for many in lengths]
    rows_spec = pl.BlockSpec((1, n, chunks, depth, width), lambda r: (r, 0, 0, 0, 0))

    def piece_spec(c, k):
        slot = places[c, k][1]
        return pl.BlockSpec((1, haps, depth, width), lambda *_: (slot, 0, 0, 0))

    normed = pl.pallas_call(
        functools.partial(pack_kernel, places),
        grid=(1,),
        in_specs=[SCALARS, whole(rows5), whole(gain_flat)],
        out_specs=[whole(shape) for shape in shapes],
        out_shape=shapes,
        compiler_params=PARAMS,
        cost_estimate=cost(PACK_COST),
        name="pack",
    )(place, rows5, gain_flat)

    def send_all(arrays):
        sent = list(arrays)
        for c, k in order:
            index, slot = places[c, k]
            if k > 0 and slot == 0:
                sent[index] = exchange(arrays[index], k)
        return sent

    state_spec = pl.BlockSpec((pairs, 1, head_dim, 2 * LANES), lambda r: (0, r, 0, 0))
    state_shape = (pairs, haps, head_dim, 2 * LANES)
    state = pl.pallas_call(
        functools.partial(row_kernel, head_dim, places),
        grid=(1,),
        in_specs=[whole(array) for array in normed] + [once(key_row)] * 2,
        out_specs=pl.BlockSpec(state_shape, lambda *_: (0, 0, 0, 0)),
        out_shape=jax.ShapeDtypeStruct(state_shape, BF16),
        compiler_params=PARAMS,
        cost_estimate=cost(ROW_COST),
        name="row",
    )(*normed, key_row, value_row)

    temper_flat = pl.pallas_call(
        functools.partial(spread_kernel, head_dim),
        grid=(1,),
        in_specs=[SCALARS],
        out_specs=whole(flat),
        out_shape=flat,
        compiler_params=PARAMS,
        cost_estimate=cost(SPREAD_COST),
        name="spread",
    )(temper)

    waiting = [places[c, k][0] for c, k in order if c > 0 and k > 1]
    held, state = lax.optimization_barrier(([normed[index] for index in waiting], state))
    queue = list(normed)
    for index, array in zip(waiting, held):
        queue[index] = array
    raw = [k > 1 for k in range(n)]
    for k in range(n):
        if raw[k]:
            queue[places[0, k][0]] = lax.dynamic_index_in_dim(
                rows5[:, :, 0], place[0] ^ k, 1, keepdims=False
            )[None]
    arrived = send_all(queue)

    shares = state.reshape(m, -1, 2 * LANES)
    shares = lax.all_to_all(shares, "pos", split_axis=0, concat_axis=0, tiled=True)

    state = None

    def add_up(shares):
        share = pl.pallas_call(
            share_kernel,
            grid=(1,),
            in_specs=[whole(shares)],
            out_specs=pl.BlockSpec(shares.shape[1:], lambda *_: (0, 0)),
            out_shape=jax.ShapeDtypeStruct(shares.shape[1:], BF16),
            compiler_params=PARAMS,
            cost_estimate=cost(SHARE_COST),
            name="share",
        )(shares)
        return lax.all_gather(share, "pos", axis=0, tiled=True).reshape(state_shape)

    one_piece = jax.ShapeDtypeStruct((1, haps, depth, width), BF16)
    one_spec = pl.BlockSpec(one_piece.shape, lambda *_: (0, 0, 0, 0))
    returned = {}
    for c in range(chunks):
        ks = [0, 1][:n] + list(range(2, n))[:: -1 if c > 0 else 1]
        blocks = [arrived[places[c, k][0]] for k in ks]
        if c > 0:
            state = add_up(shares)
            blocks, state = lax.optimization_barrier((blocks, state))
        every = pltpu.VMEM((haps * n, depth, width), BF16)
        results = pl.pallas_call(
            functools.partial(column_kernel, head_dim, [raw[k] and c == 0 for k in ks]),
            grid=(1,),
            in_specs=[whole(temper_flat), whole(gain_flat)]
            + [once(query_col)] * 3
            + [piece_spec(c, k) for k in ks],
            out_specs=[one_spec] * n,
            out_shape=[one_piece] * n,
            scratch_shapes=[every] * 3,
            compiler_params=PARAMS,
            cost_estimate=cost(COLUMN_COSTS[c]),
            name="column",
        )(temper_flat, gain_flat, query_col, key_col, value_col, *blocks)
        if c > 0 and n > 1:
            results, returned[0, 1] = lax.optimization_barrier((results, returned[0, 1]))
        for k, result in zip(ks, results):
            returned[c, k] = exchange(result, k) if k > 0 else result

    if state is None:
        state = add_up(shares)
    acc = pl.pallas_call(
        functools.partial(along_kernel, head_dim, order),
        grid=(haps,),
        in_specs=[SCALARS, rows_spec, whole(gain_flat), once(query_row), state_spec, whole(head_gain_flat), once(out_row)],
        out_specs=pl.BlockSpec((1, len(order), depth, width), lambda r: (r, 0, 0, 0)),
        out_shape=jax.ShapeDtypeStruct((haps, len(order), depth, width), F32),
        scratch_shapes=[pltpu.VMEM((length, width), BF16)],
        compiler_params=PARAMS,
        cost_estimate=cost(ALONG_COST),
        name="along",
    )(place, rows5, gain_flat, query_row, state, head_gain_flat, out_row)

    groups = [[], [], []]
    for c, k in order:
        groups[2 if c == chunks - 1 and k > 1 else 0 if c == 0 and chunks > 1 else 1].append((c, k))
    updated = None
    for pieces, weight in zip(groups, FINISH_COSTS):
        if not pieces:
            continue
        pieces = pieces[::-1]
        extra = [] if updated is None else [updated]
        count = len(pieces)
        updated = pl.pallas_call(
            functools.partial(finish_kernel, pieces, order),
            grid=(1,),
            in_specs=[SCALARS, anywhere, once(out_col)]
            + [one_spec] * count
            + [anywhere] * len(extra),
            out_specs=anywhere,
            out_shape=jax.ShapeDtypeStruct(rows5.shape, BF16),
            scratch_shapes=[
                pltpu.VMEM((count, haps, depth, width), F32),
                pltpu.VMEM((count, haps, depth, width), BF16),
                pltpu.SemaphoreType.DMA((count,)),
                pltpu.SemaphoreType.DMA((count,)),
            ],
            input_output_aliases={3 + count: 0} if extra else {},
            compiler_params=PARAMS,
            cost_estimate=cost(weight),
            name="finish",
        )(place, acc, out_col, *[returned[piece] for piece in pieces], *extra)
    return updated.reshape(haps, length, width)


def solution(mesh):
    sizes = (mesh.shape["hap"], mesh.shape["pos"])
    return jax.shard_map(
        functools.partial(local, sizes),
        mesh=mesh,
        in_specs=(P("hap", "pos", None), P(), P(), P(), P(), P(), P(), P(), P(), P(), P(), P()),
        out_specs=P("hap", "pos", None),
        check_vma=False,
    )
```

```python
import functools

import jax
import jax.numpy as jnp
from jax import lax
from jax.experimental import pallas as pl
from jax.experimental.pallas import tpu as pltpu
from jax.sharding import PartitionSpec as P

EPS = 1e-06
LANES = 128
TILE = 16
F32 = jnp.float32
BF16 = jnp.bfloat16
VMEM_MIB = 24
PACK_COST = 10
ROW_COST = 20
SPREAD_COST = 5
SHARE_COST = 5
ALONG_COST = 0
COLUMN_COSTS = (200, 30)
FINISH_COSTS = (30, 0, 0)


def last_dims(left, right):
    return lax.dot_general(left, right, (((1,), (1,)), ((), ())), preferred_element_type=F32)


def first_dims(left, right):
    return lax.dot_general(left, right, (((0,), (0,)), ((), ())), preferred_element_type=F32)


def plain(left, right):
    return jnp.dot(left, right, preferred_element_type=F32)


def lane_of(shape):
    return lax.broadcasted_iota(jnp.int32, shape, len(shape) - 1)


def group_ones(size, head_dim):
    rows = lax.broadcasted_iota(jnp.int32, (size, size), 0) // head_dim
    cols = lax.broadcasted_iota(jnp.int32, (size, size), 1) // head_dim
    return jnp.where(rows == cols, 1.0, 0.0).astype(BF16)


def head_square_sums(values, ones):
    size = ones.shape[0]
    parts = []
    for start in range(0, values.shape[1], size):
        piece = values[:, start : start + size]
        square = piece * piece
        high = square.astype(BF16)
        low = (square - high.astype(F32)).astype(BF16)
        parts.append(plain(high, ones) + plain(low, ones))
    return jnp.concatenate(parts, axis=1) if len(parts) > 1 else parts[0]


def feature_pair(values):
    small = jnp.exp(-jnp.abs(values))
    up = values > 0
    plus = jnp.where(up, values + 1.0, small).astype(BF16)
    minus = jnp.where(up, small, 1.0 - values).astype(BF16)
    return plus, minus


def normalise(rows, gain):
    wide = rows.astype(F32)
    scale = lax.rsqrt(jnp.mean(wide * wide, axis=-1, keepdims=True) + EPS)
    return (wide * scale * gain).astype(BF16)


def spread_kernel(head_dim, temper_ref, out_ref):
    for head in range(temper_ref.shape[0]):
        out_ref[:, head * head_dim : (head + 1) * head_dim] = jnp.full(
            (1, head_dim), temper_ref[head], F32
        )


def pack_kernel(places, place_ref, rows_ref, gain_ref, *outs):
    z = place_ref[0]
    gain = gain_ref[...]
    for (c, k), (index, slot) in places.items():
        for r in range(rows_ref.shape[0]):
            outs[index][slot, r] = normalise(rows_ref[r, z ^ k, c], gain)


def share_kernel(shares_ref, out_ref):
    total = shares_ref[0].astype(F32)
    for i in range(1, shares_ref.shape[0]):
        total = total + shares_ref[i].astype(F32)
    out_ref[...] = total.astype(BF16)


def row_kernel(head_dim, places, *refs):
    wk_ref, wv_ref, state_ref = refs[-3:]
    haps = state_ref.shape[1]
    rows = jnp.concatenate(
        [refs[index][slot, r] for r in range(haps) for index, slot in places.values()], axis=0
    )
    length = rows.shape[0] // haps
    keys = plain(rows, wk_ref[...]).astype(BF16)
    values = plain(rows, wv_ref[...]).astype(BF16)
    first_head = lane_of((head_dim, 2 * LANES)) % LANES < head_dim
    for r in range(haps):
        here = slice(r * length, (r + 1) * length)
        for pair in range(keys.shape[1] // LANES):
            lanes = slice(pair * LANES, (pair + 1) * LANES)
            plus, minus = feature_pair(keys[here, lanes].astype(F32))
            features = jnp.concatenate([plus, minus], axis=1)
            state = first_dims(values[here, lanes], features)
            folded = jnp.where(first_head, state[:head_dim], state[head_dim:])
            state_ref[pair, r] = folded.astype(BF16)


def along_kernel(
    head_dim, order, place_ref, rows_ref, norm_ref, wq_ref, state_ref, gain_ref, wo_ref, out_ref, mixed
):
    z = place_ref[0]
    rows = jnp.concatenate([rows_ref[0, z ^ k, c] for c, k in order], axis=0)
    queries = plain(normalise(rows, norm_ref[...]), wq_ref[...]).astype(BF16)
    first_head = lane_of((head_dim, 2 * LANES)) % LANES < head_dim
    ones = group_ones(2 * LANES, head_dim)
    alongs = []
    for pair in range(state_ref.shape[0]):
        lower = pair * LANES
        plus, minus = feature_pair(queries[:, lower : lower + LANES].astype(F32))
        features = jnp.concatenate([plus, minus], axis=1)
        folded = state_ref[pair, 0]
        none = jnp.zeros_like(folded)
        state = jnp.concatenate(
            [jnp.where(first_head, folded, none), jnp.where(first_head, none, folded)], axis=0
        )
        alongs.append(last_dims(features, state))
        if pair % 2 == 1:
            lower -= LANES
            wide = jnp.concatenate(alongs[-2:], axis=1)
            mean = head_square_sums(wide, ones) * (1.0 / head_dim)
            scaled = wide * lax.rsqrt(mean + EPS) * gain_ref[:, lower : lower + 2 * LANES]
            mixed[:, lower : lower + 2 * LANES] = scaled.astype(BF16)
    row_out = plain(mixed[...], wo_ref[...])
    depth = rows_ref.shape[3]
    for i, (c, k) in enumerate(order):
        out_ref[0, i] = rows_ref[0, z ^ k, c].astype(F32) + row_out[i * depth : (i + 1) * depth]


def column_kernel(head_dim, raw, temper_ref, gain_ref, wq_ref, wk_ref, wv_ref, *refs):
    count = len(raw)
    blocks = refs[:count]
    outs = refs[-3 - count : -3]
    q_all, k_all, v_all = refs[-3:]
    _one, haps, depth, width = blocks[0].shape
    pieces = []
    for block, is_raw in zip(blocks, raw):
        piece = block[0].reshape(haps * depth, width)
        pieces.append(normalise(piece, gain_ref[...]) if is_raw else piece)
    rows = jnp.concatenate(pieces, axis=0)
    shape = q_all.shape
    ones = group_ones(2 * LANES, head_dim)
    q = plain(rows, wq_ref[...]).astype(BF16).astype(F32)
    q = q * lax.rsqrt(head_square_sums(q, ones) + EPS) * temper_ref[...]
    q_all[...] = q.astype(BF16).reshape(shape)
    k = plain(rows, wk_ref[...]).astype(BF16).astype(F32)
    k = k * lax.rsqrt(head_square_sums(k, ones) + EPS)
    k_all[...] = k.astype(BF16).reshape(shape)
    v_all[...] = plain(rows, wv_ref[...]).astype(BF16).reshape(shape)
    all_haps = shape[0]
    many = all_haps * TILE
    same = (
        lax.broadcasted_iota(jnp.int32, (2 * many, many), 0) % TILE
        == lax.broadcasted_iota(jnp.int32, (2 * many, many), 1) % TILE
    )
    first_head = lane_of((many, LANES)) < head_dim
    none = jnp.zeros((many, LANES), BF16)
    one = jnp.ones((many, LANES), BF16)
    for start in range(0, depth, TILE):
        for lower in range(0, width, LANES):
            at = (slice(None), slice(start, start + TILE), slice(lower, lower + LANES))
            query = q_all[at].reshape(many, LANES)
            key = k_all[at].reshape(many, LANES)
            value = v_all[at].reshape(many, LANES)
            queries = jnp.concatenate(
                [jnp.where(first_head, query, none), jnp.where(first_head, none, query)], axis=0
            )
            weight = jnp.where(same, jnp.exp(last_dims(queries, key)), 0.0).astype(BF16)
            sums = plain(weight, jnp.concatenate([value, one], axis=1))
            summed = jnp.where(first_head, sums[:many, :LANES], sums[many:, :LANES])
            total = jnp.where(first_head, sums[:many, LANES:], sums[many:, LANES:])
            result = (summed / total).astype(BF16).reshape(all_haps, TILE, LANES)
            for k in range(count):
                outs[k][0, :, start : start + TILE, lower : lower + LANES] = result[
                    k * haps : (k + 1) * haps
                ]


def finish_kernel(pieces, order, place_ref, acc_ref, wo_ref, *refs):
    mixed = refs[: len(pieces)]
    out_ref, result, out_sems = refs[-3:]
    z = place_ref[0]
    _one, haps, depth, _width = mixed[0].shape
    flat = jnp.concatenate([block[0, r] for block in mixed for r in range(haps)], axis=0)
    col_out = plain(flat, wo_ref[...])
    stores = []
    for i, (c, k) in enumerate(pieces):
        for r in range(haps):
            lower = (i * haps + r) * depth
            result[i, r] = (acc_ref[r, order.index((c, k))] + col_out[lower : lower + depth]).astype(BF16)
        store = pltpu.make_async_copy(result.at[i], out_ref.at[:, z ^ k, c], out_sems.at[i])
        store.start()
        stores.append(store)
    for store in stores:
        store.wait()


def whole(array):
    zeros = (0,) * array.ndim
    return pl.BlockSpec(array.shape, lambda *_: zeros)


def once(array):
    zeros = (0,) * array.ndim
    return pl.BlockSpec(array.shape, lambda *_: zeros, pipeline_mode=pl.Buffered(1))


SCALARS = pl.BlockSpec(memory_space=pltpu.SMEM)
PARAMS = pltpu.CompilerParams(vmem_limit_bytes=VMEM_MIB * 1024 * 1024)


def cost(micros):
    return pl.CostEstimate(flops=int(micros * 1e9), bytes_accessed=1, transcendentals=0)


def local(
    sizes,
    haplo_rows,
    norm_gain,
    query_row,
    key_row,
    value_row,
    out_row,
    head_gain,
    query_col,
    key_col,
    value_col,
    out_col,
    temper,
):
    n, m = sizes
    haps, length, width = haplo_rows.shape
    heads = temper.shape[0]
    head_dim = width // heads
    owned = length // n
    chunks = 2 if owned % (2 * TILE) == 0 else 1
    depth = owned // chunks
    pairs = width // LANES
    place = lax.axis_index("hap").astype(jnp.int32)[None]
    rows5 = haplo_rows.reshape(haps, n, chunks, depth, width)
    gain_flat = norm_gain[None, :]
    head_gain_flat = head_gain[None, :]
    flat = jax.ShapeDtypeStruct((1, width), F32)
    anywhere = pl.BlockSpec(memory_space=pl.ANY)

    def exchange(array, k):
        return lax.ppermute(array, "hap", [(i, i ^ k) for i in range(n)])

    order = [(c, k) for c in range(chunks) for k in range(n)]
    places, lengths = {}, []
    for c, k in order:
        if k == 1 and c > 0:
            places[c, k] = (places[0, 1][0], c)
        else:
            places[c, k] = (len(lengths), 0)
            lengths.append(chunks if k == 1 else 1)
    shapes = [jax.ShapeDtypeStruct((many, haps, depth, width), BF16) for many in lengths]
    rows_spec = pl.BlockSpec((1, n, chunks, depth, width), lambda r: (r, 0, 0, 0, 0))

    def piece_spec(c, k):
        slot = places[c, k][1]
        return pl.BlockSpec((1, haps, depth, width), lambda *_: (slot, 0, 0, 0))

    normed = pl.pallas_call(
        functools.partial(pack_kernel, places),
        grid=(1,),
        in_specs=[SCALARS, whole(rows5), whole(gain_flat)],
        out_specs=[whole(shape) for shape in shapes],
        out_shape=shapes,
        compiler_params=PARAMS,
        cost_estimate=cost(PACK_COST),
        name="pack",
    )(place, rows5, gain_flat)

    def send_all(arrays):
        sent = list(arrays)
        for c, k in order:
            index, slot = places[c, k]
            if k > 0 and slot == 0:
                sent[index] = exchange(arrays[index], k)
        return sent

    state_spec = pl.BlockSpec((pairs, 1, head_dim, 2 * LANES), lambda r: (0, r, 0, 0))
    state_shape = (pairs, haps, head_dim, 2 * LANES)
    state = pl.pallas_call(
        functools.partial(row_kernel, head_dim, places),
        grid=(1,),
        in_specs=[whole(array) for array in normed] + [once(key_row)] * 2,
        out_specs=pl.BlockSpec(state_shape, lambda *_: (0, 0, 0, 0)),
        out_shape=jax.ShapeDtypeStruct(state_shape, BF16),
        compiler_params=PARAMS,
        cost_estimate=cost(ROW_COST),
        name="row",
    )(*normed, key_row, value_row)

    temper_flat = pl.pallas_call(
        functools.partial(spread_kernel, head_dim),
        grid=(1,),
        in_specs=[SCALARS],
        out_specs=whole(flat),
        out_shape=flat,
        compiler_params=PARAMS,
        cost_estimate=cost(SPREAD_COST),
        name="spread",
    )(temper)

    waiting = [places[c, k][0] for c, k in order if c > 0 and k > 1]
    held, state = lax.optimization_barrier(([normed[index] for index in waiting], state))
    queue = list(normed)
    for index, array in zip(waiting, held):
        queue[index] = array
    raw = [k > 1 for k in range(n)]
    for k in range(n):
        if raw[k]:
            queue[places[0, k][0]] = lax.dynamic_index_in_dim(
                rows5[:, :, 0], place[0] ^ k, 1, keepdims=False
            )[None]
    arrived = send_all(queue)

    shares = state.reshape(m, -1, 2 * LANES)
    shares = lax.all_to_all(shares, "pos", split_axis=0, concat_axis=0, tiled=True)

    state = None

    def add_up(shares):
        share = pl.pallas_call(
            share_kernel,
            grid=(1,),
            in_specs=[whole(shares)],
            out_specs=pl.BlockSpec(shares.shape[1:], lambda *_: (0, 0)),
            out_shape=jax.ShapeDtypeStruct(shares.shape[1:], BF16),
            compiler_params=PARAMS,
            cost_estimate=cost(SHARE_COST),
            name="share",
        )(shares)
        return lax.all_gather(share, "pos", axis=0, tiled=True).reshape(state_shape)

    one_piece = jax.ShapeDtypeStruct((1, haps, depth, width), BF16)
    one_spec = pl.BlockSpec(one_piece.shape, lambda *_: (0, 0, 0, 0))
    returned = {}
    for c in range(chunks):
        ks = [0, 1][:n] + list(range(2, n))[:: -1 if c > 0 else 1]
        blocks = [arrived[places[c, k][0]] for k in ks]
        if c > 0:
            state = add_up(shares)
            blocks, state = lax.optimization_barrier((blocks, state))
        every = pltpu.VMEM((haps * n, depth, width), BF16)
        results = pl.pallas_call(
            functools.partial(column_kernel, head_dim, [raw[k] and c == 0 for k in ks]),
            grid=(1,),
            in_specs=[whole(temper_flat), whole(gain_flat)]
            + [once(query_col)] * 3
            + [piece_spec(c, k) for k in ks],
            out_specs=[one_spec] * n,
            out_shape=[one_piece] * n,
            scratch_shapes=[every] * 3,
            compiler_params=PARAMS,
            cost_estimate=cost(COLUMN_COSTS[c]),
            name="column",
        )(temper_flat, gain_flat, query_col, key_col, value_col, *blocks)
        if c > 0 and n > 1:
            results, returned[0, 1] = lax.optimization_barrier((results, returned[0, 1]))
        for k, result in zip(ks, results):
            returned[c, k] = exchange(result, k) if k > 0 else result

    if state is None:
        state = add_up(shares)
    acc = pl.pallas_call(
        functools.partial(along_kernel, head_dim, order),
        grid=(haps,),
        in_specs=[SCALARS, rows_spec, whole(gain_flat), once(query_row), state_spec, whole(head_gain_flat), once(out_row)],
        out_specs=pl.BlockSpec((1, len(order), depth, width), lambda r: (r, 0, 0, 0)),
        out_shape=jax.ShapeDtypeStruct((haps, len(order), depth, width), F32),
        scratch_shapes=[pltpu.VMEM((length, width), BF16)],
        compiler_params=PARAMS,
        cost_estimate=cost(ALONG_COST),
        name="along",
    )(place, rows5, gain_flat, query_row, state, head_gain_flat, out_row)

    groups = [[], [], []]
    for c, k in order:
        groups[2 if c == chunks - 1 and k > 1 else 0 if c == 0 and chunks > 1 else 1].append((c, k))
    updated = None
    for pieces, weight in zip(groups, FINISH_COSTS):
        if not pieces:
            continue
        pieces = pieces[::-1]
        extra = [] if updated is None else [updated]
        count = len(pieces)
        updated = pl.pallas_call(
            functools.partial(finish_kernel, pieces, order),
            grid=(1,),
            in_specs=[SCALARS, once(acc), once(out_col)]
            + [one_spec] * count
            + [anywhere] * len(extra),
            out_specs=anywhere,
            out_shape=jax.ShapeDtypeStruct(rows5.shape, BF16),
            scratch_shapes=[
                pltpu.VMEM((count, haps, depth, width), BF16),
                pltpu.SemaphoreType.DMA((count,)),
            ],
            input_output_aliases={3 + count: 0} if extra else {},
            compiler_params=PARAMS,
            cost_estimate=cost(weight),
            name="finish",
        )(place, acc, out_col, *[returned[piece] for piece in pieces], *extra)
    return updated.reshape(haps, length, width)


def solution(mesh):
    sizes = (mesh.shape["hap"], mesh.shape["pos"])
    return jax.shard_map(
        functools.partial(local, sizes),
        mesh=mesh,
        in_specs=(P("hap", "pos", None), P(), P(), P(), P(), P(), P(), P(), P(), P(), P(), P()),
        out_specs=P("hap", "pos", None),
        check_vma=False,
    )
```
